1024 devices in a mesh: node: 256 (over y, x, z_lo, core), local: 4 (over z_hi).
Axes of the slice: x: 4, y: 8, z: 16 (z_hi: 4, z_lo: 4; z = z_hi * 4 + z_lo), core: 2. Of those that a mesh axis runs over, the one named last changes fastest.
Arguments:
- tokens: bfloat16 [131072, 4096], P(('node', 'local')), may hold values from -24 to 24
- queries: bfloat16 [131072, 4096], P(('node', 'local')), may hold values from -6 to 6
- keys: bfloat16 [131072, 512], P(('node', 'local')), may hold values from -6 to 6
- grad_attended: bfloat16 [131072, 4096], P(('node', 'local')), may hold values from -6 to 6
- w_value: bfloat16 [4096, 512], P('local'), may hold values from -0.09375 to 0.09375
Outputs:
- d_keys: bfloat16 [131072, 512], P(('node', 'local'))
- grad_value: float32 [4096, 512], P(('local', 'node'))
The draws below stay inside these ranges and needn't reach their ends.
All inputs are finite; a program needn't handle non-finite values.
Results may differ from the reference program's by a relative error of at most 0.018.
Values may be sent and summed in bfloat16 or wider, within the bound.
A program may use at most 32 MiB of HBM per device.

```python
import jax
import jax.numpy as jnp
from jax import lax

D = 4096
HD = 128
KVH = 4
GROUP = 8
TOK_DEV = 128
KW = 512
QW = 4096
TOKENS = 131072
N_NODE = 256
N_LOCAL = 4


def draw_queries(key, part):
    key = jax.random.fold_in(key, 5)
    entries = jax.random.truncated_normal(key, -4.0, 4.0, (TOKENS, KVH * GROUP * HD), jnp.float32)
    return entries.astype(jnp.bfloat16)


def draw_keys(key, part):
    key = jax.random.fold_in(key, 7)
    entries = jax.random.truncated_normal(key, -4.0, 4.0, (TOKENS, KVH * HD), jnp.float32)
    return entries.astype(jnp.bfloat16)


def spiked(values, own_key, source, target, shards_of, factor):
    owner, partner = [(jnp.arange(values.shape[dim]) // (values.shape[dim] // shards_of)).reshape([-1 if axis == dim else 1 for axis in range(values.ndim)]) for dim in (source, target)]
    chosen = jax.random.permutation(own_key, shards_of)[partner]
    strong = (owner == chosen) | (owner == (partner + shards_of // 2) % shards_of)
    return jnp.where(strong, factor * values, values)


def block_scale(stream_key, shape, shards, smallest, high):
    def one(dim, shards_of):
        heights = jax.random.uniform(jax.random.fold_in(jax.random.fold_in(stream_key, 6), dim), (shards_of,), jnp.float32, smallest / len(shards), high / len(shards))
        return jnp.repeat(jnp.exp(heights), shape[dim] // shards_of).reshape((-1,) + (1,) * (len(shape) - dim - 1))

    level = one(*shards[0])
    for cut in shards[1:]:
        level = level * one(*cut)
    return level


def noise(key, extent, scale, bound, pieces=(), kind=jnp.bfloat16):
    factor_of = block_scale(key, extent, pieces, -0.22, 0.18) if pieces else 1.0
    values = jax.random.normal(key, extent, jnp.float32) * scale * factor_of
    return jnp.minimum(jnp.maximum(values, -bound), bound).astype(kind)


def heavy_noise(own_key, dims, scale, reach, cuts, heavy, held_as=jnp.bfloat16):
    array = scale * jax.random.normal(own_key, dims, jnp.float32)
    if cuts:
        array = array * block_scale(own_key, dims, cuts, -0.22, 0.18)
    return jnp.clip(spiked(array, jax.random.fold_in(own_key, 3), *heavy), -reach, reach).astype(held_as)


def setup_inputs(seed: int = 0) -> dict:
    splits = jax.random.split(jax.random.key(seed), 6)
    tokens = heavy_noise(splits[0], (TOKENS, D), 1.0, 24.0, ((0, 1024),), (0, 1, 1024, 6.0))
    queries = draw_queries(jax.random.fold_in(splits[5], 71), 0)
    keys = draw_keys(jax.random.fold_in(splits[5], 71), 0)
    grad_attended = noise(splits[3], (TOKENS, QW), 1.0, 6.0, ((0, 1024),))
    w_value = noise(splits[4], (D, KW), D ** -0.5, 0.09375, ((0, 4),))
    return dict(tokens=tokens, queries=queries, keys=keys, grad_attended=grad_attended, w_value=w_value)


def reference(tokens, queries, keys, grad_attended, w_value):
    sequences = N_NODE * N_LOCAL
    width = KVH * HD
    loss_scale = float(TOKENS) ** -0.5
    head_scale = float(HD) ** -0.5
    row_ids = lax.broadcasted_iota(jnp.int32, (TOK_DEV, TOK_DEV), 0)
    col_ids = lax.broadcasted_iota(jnp.int32, (TOK_DEV, TOK_DEV), 1)
    causal = (col_ids <= row_ids)[None, None]

    def one_sequence(total, blocks):
        token_rows, query_rows, key_rows, upper_rows = blocks
        values = jnp.dot(token_rows, w_value, preferred_element_type=jnp.float32).astype(jnp.bfloat16)
        query_heads = query_rows.astype(jnp.float32).reshape(TOK_DEV, KVH, GROUP, HD)
        key_heads = key_rows.astype(jnp.float32).reshape(TOK_DEV, KVH, HD)
        value_heads = values.astype(jnp.float32).reshape(TOK_DEV, KVH, HD)
        upper_heads = upper_rows.astype(jnp.float32).reshape(TOK_DEV, KVH, GROUP, HD)
        scores = jnp.einsum("tagd,sad->agts", query_heads, key_heads) * head_scale
        scores = jnp.where(causal, scores, jnp.float32(-1e30))
        row_peak = jnp.max(scores, axis=-1, keepdims=True)
        raised = jnp.exp(scores - row_peak)
        soft_weights = (raised / jnp.sum(raised, axis=-1, keepdims=True)).astype(jnp.bfloat16)
        soft_float = soft_weights.astype(jnp.float32)
        grad_probs = jnp.einsum("tagd,sad->agts", upper_heads, value_heads)
        delta = jnp.sum(soft_float * grad_probs, axis=-1, keepdims=True)
        grad_scores = (soft_float * (grad_probs - delta)).astype(jnp.bfloat16).astype(jnp.float32)
        d_keys = jnp.einsum("agts,tagd->sad", grad_scores, query_heads) * head_scale
        d_keys = d_keys.astype(jnp.bfloat16).reshape(TOK_DEV, width)
        grad_values = jnp.einsum("agts,tagd->sad", soft_float, upper_heads)
        grad_values = grad_values.astype(jnp.bfloat16).reshape(TOK_DEV, width)
        term = jnp.dot(token_rows.T, grad_values, preferred_element_type=jnp.float32) * loss_scale
        term = lax.optimization_barrier(term.astype(jnp.bfloat16)).astype(jnp.float32)
        return total + term, d_keys

    start = jnp.zeros((D, width), jnp.float32)
    blocks = (tokens.reshape(sequences, TOK_DEV, D), queries.reshape(sequences, TOK_DEV, KVH * GROUP * HD),
              keys.reshape(sequences, TOK_DEV, width), grad_attended.reshape(sequences, TOK_DEV, KVH * GROUP * HD))
    grad_value, d_keys = lax.scan(one_sequence, start, blocks)
    return d_keys.reshape(TOKENS, width), grad_value
```

```python
import jax
import jax.numpy as jnp
from jax import lax
from jax.experimental import pallas as pl
from jax.experimental.pallas import tpu as pltpu
from jax.sharding import PartitionSpec as P

HD = 128
KVH = 4
GROUP = 8
ROWS = 128
KW = 512
NX, NY, NZL, NZH, NC = 4, 8, 4, 4, 2
NG = NX * NC
MESH = pl.DeviceIdType.MESH
F32 = jnp.float32
BF16 = jnp.bfloat16


def node_of(y, x, z_lo, core):
    return ((y * NX + x) * NZL + z_lo) * NC + core


def over_rows(left, right):
    return lax.dot_general(left, right, (((0,), (0,)), ((), ())), preferred_element_type=F32)


def over_columns(left, right):
    return lax.dot_general(left, right, (((1,), (1,)), ((), ())), preferred_element_type=F32)


def stacked(ref, a):
    return jnp.concatenate(
        [ref[:, (a * GROUP + g) * HD : (a * GROUP + g + 1) * HD] for g in range(GROUP)], axis=0
    )


def kernel(
    tok_hbm, q_hbm, k_hbm, g_hbm, w_hbm, dk_ref, gw_ref,
    tok, q, k, g, w_own, w_far, soft, tok_group, gv_group, part_send, part_recv,
    fin_send, fin_recv, load_sem, send_sem, recv_sem, *, loss_scale,
):
    node, z_hi = lax.axis_index("node"), lax.axis_index("local")
    core = lax.rem(node, NC)
    z_lo = lax.rem(node // NC, NZL)
    x = lax.rem(node // (NC * NZL), NX)
    y = node // (NC * NZL * NX)
    z = z_hi * NZL + z_lo
    p = x * NC + core
    head_scale = float(HD) ** -0.5

    def device(y_, x_, core_):
        return (node_of(y_, x_, z_lo, core_), z_hi)

    sibling = device(y, x, 1 - core)
    x_peers = [lax.rem(x + d, NX) for d in range(1, NX)]
    y_peers = [lax.rem(y + d, NY) for d in range(1, NY)]
    far_peers = [lax.rem(z_hi + d, NZH) for d in range(1, NZH)]

    loads = [
        pltpu.make_async_copy(src, dst, load_sem.at[i])
        for i, (src, dst) in enumerate(
            [(q_hbm, q), (k_hbm, k), (g_hbm, g), (tok_hbm, tok), (w_hbm, w_own)]
        )
    ]
    for load in loads:
        load.start()

    barrier = pltpu.get_barrier_semaphore()

    def greet(device_id):
        pl.semaphore_signal(barrier, inc=1, device_id=device_id, device_id_type=MESH)

    greet(sibling)
    for x_ in x_peers:
        for core_ in (core, 1 - core):
            greet(device(y, x_, core_))
    for y_ in y_peers:
        greet(device(y_, x, core))
    for h in far_peers:
        greet((node, h))
    giver_y, giver_x, giver_core = x * 2 + z_lo // 2, y // 2, lax.rem(y, 2)
    takes_own = (giver_y == y) & (giver_x == x) & (giver_core == core)
    for z_ in range(NZH * NZL):
        giver = (node_of(giver_y, giver_x, z_ % NZL, giver_core), z_ // NZL)

        @pl.when(jnp.logical_not(takes_own & (z == z_)))
        def _():
            greet(giver)

    near = 1 + 2 * (NX - 1) + (NY - 1) + (NZH - 1)
    pl.semaphore_wait(barrier, near + NZH * NZL - jnp.where(takes_own, 1, 0))

    def send(src, dst, phase, device_id):
        pltpu.make_async_remote_copy(
            src_ref=src, dst_ref=dst, send_sem=send_sem.at[phase], recv_sem=recv_sem.at[phase],
            device_id=device_id, device_id_type=MESH,
        ).start()

    def wait(ref, sem):
        pltpu.make_async_copy(ref, ref, sem).wait()

    W_Z, W_Y, W_X, W_C, TOK, GV_X, GV_OWN, GV_C, PART, FIN = range(10)

    piece = (core * NX + x) * NY + y
    for d, h in enumerate(far_peers):
        send(
            w_hbm.at[pl.ds(pl.multiple_of(piece * 16, 16), 16)],
            w_far.at[piece, NZH - 2 - d], W_Z, (node, h),
        )

    def columns(zh, p_):
        return tok_hbm.at[:, pl.ds(pl.multiple_of(zh * (NG * HD) + p_ * HD, HD), HD)]

    for x_, core_ in [(x, 1 - core)] + [(x_, c_) for x_ in x_peers for c_ in (core, 1 - core)]:
        for zh in range(NZH):
            send(
                columns(zh, x_ * NC + core_), tok_group.at[p, :, zh * HD : (zh + 1) * HD], TOK,
                device(y, x_, core_),
            )
    for zh in range(NZH):
        pltpu.make_async_copy(
            columns(zh, p), tok_group.at[p, :, zh * HD : (zh + 1) * HD], recv_sem.at[TOK]
        ).start()

    row_ids = lax.broadcasted_iota(jnp.int32, (GROUP, ROWS, ROWS), 1).reshape(GROUP * ROWS, ROWS)
    col_ids = lax.broadcasted_iota(jnp.int32, (GROUP * ROWS, ROWS), 1)
    allowed = col_ids <= row_ids

    def softmax_head(a):
        cols = slice(a * HD, (a + 1) * HD)
        scores = over_columns(stacked(q, a), k[:, cols]) * head_scale
        scores = jnp.where(allowed, scores, F32(-1e30))
        raised = jnp.exp(scores - jnp.max(scores, axis=-1, keepdims=True))
        weights = (raised / jnp.sum(raised, axis=-1, keepdims=True)).astype(BF16)
        soft[a] = weights
        gv_group[p, :, cols] = over_rows(weights, stacked(g, a)).astype(BF16)

    for load in loads[:3]:
        load.wait()
    softmax_head(0)
    softmax_head(1)
    wait(w_far.at[0], recv_sem.at[W_Z])
    for y_ in y_peers:
        send(w_far.at[piece], w_far.at[piece], W_Y, device(y_, x, core))
    softmax_head(2)
    softmax_head(3)

    for x_ in x_peers:
        send(gv_group.at[p], gv_group.at[p], GV_X, device(y, x_, core))
    send(gv_group.at[p], gv_group.at[p], GV_OWN, sibling)
    wait(w_far.at[0 : NY - 1], recv_sem.at[W_Y])
    plane = pl.ds((core * NX + x) * NY, NY)
    for x_ in x_peers:
        send(w_far.at[plane], w_far.at[plane], W_X, device(y, x_, core))
    loads[3].wait()
    loads[4].wait()
    own_columns = pl.ds(pl.multiple_of(z_hi * (NG * HD), HD), NG * HD)
    total = jnp.dot(tok[:, own_columns], w_own[...], preferred_element_type=F32)
    wait(gv_group.at[0 : NX - 1], recv_sem.at[GV_X])
    for x_ in x_peers:
        send(gv_group.at[x_ * NC + core], gv_group.at[x_ * NC + core], GV_C, sibling)
    wait(tok_group, recv_sem.at[TOK])
    wait(gv_group.at[0], recv_sem.at[GV_OWN])
    wait(gv_group.at[0 : NX - 1], recv_sem.at[GV_C])

    gv_all = gv_group[...].reshape(NG * ROWS, KW)
    for zh in range(NZH):
        lanes = slice(zh * HD, (zh + 1) * HD)
        tok_all = tok_group[:, :, lanes].reshape(NG * ROWS, HD)
        term = over_rows(tok_all, gv_all) * loss_scale
        part_send[:, zh] = term.astype(BF16).reshape(NY, 16, KW)
    for y_ in y_peers:
        send(part_send.at[y_], part_recv.at[y], PART, device(y_, x, core))
    pltpu.make_async_copy(part_send.at[y], part_recv.at[y], recv_sem.at[PART]).start()
    wait(part_recv, recv_sem.at[PART])
    part = part_recv[0].astype(F32)
    for y_ in range(1, NY):
        part = part + part_recv[y_].astype(F32)
    part = part.reshape(64, KW)
    for j in range(16):
        fin_send[j] = part[4 * j : 4 * j + 4]
    gives_own = (lax.rem(y, 2) == z_lo // 2) & (y // 2 == x) & (x * NC + core == y)
    for j in range(16):
        zh, zl1, core_ = j // 4, (j // 2) % 2, j % 2
        z_lo_ = lax.rem(y, 2) * 2 + zl1
        owner = (node_of(x * NC + core, y // 2, z_lo_, core_), zh)
        own = gives_own & (z_hi == zh) & (z_lo == z_lo_) & (core == core_)

        @pl.when(own)
        def _():
            pltpu.make_async_copy(fin_send.at[j], fin_recv.at[z], recv_sem.at[FIN]).start()

        @pl.when(jnp.logical_not(own))
        def _():
            send(fin_send.at[j], fin_recv.at[z], FIN, owner)

    wait(w_far.at[0 : (NX - 1) * NY], recv_sem.at[W_X])
    half = pl.ds(core * (NX * NY), NX * NY)
    send(w_far.at[half], w_far.at[half], W_C, sibling)
    wait(w_far.at[0 : NX * NY], recv_sem.at[W_C])
    for d in range(NZH - 1):
        h = far_peers[d]
        cols = pl.ds(pl.multiple_of(h * (NG * HD), HD), NG * HD)
        w_h = w_far[:, d].reshape(NG * HD, KW)
        total = total + jnp.dot(tok[:, cols], w_h, preferred_element_type=F32)
    values = total.astype(BF16)
    for a in range(KVH):
        cols = slice(a * HD, (a + 1) * HD)
        grad_probs = over_columns(stacked(g, a), values[:, cols])
        soft_float = soft[a].astype(F32)
        delta = jnp.sum(soft_float * grad_probs, axis=-1, keepdims=True)
        grad_scores = (soft_float * (grad_probs - delta)).astype(BF16)
        dk_ref[:, cols] = (over_rows(grad_scores, stacked(q, a)) * head_scale).astype(BF16)

    wait(fin_recv, recv_sem.at[FIN])
    out = fin_recv[0]
    for z_ in range(1, NZH * NZL):
        out = out + fin_recv[z_]
    gw_ref[...] = out

    wait(w_far.at[0], send_sem.at[W_Z])
    wait(w_far.at[0 : NY - 1], send_sem.at[W_Y])
    wait(w_far.at[0 : (NX - 1) * NY], send_sem.at[W_X])
    wait(w_far.at[0 : NX * NY], send_sem.at[W_C])
    wait(tok_group.at[0 : NG - 1], send_sem.at[TOK])
    wait(gv_group.at[0 : NX - 1], send_sem.at[GV_X])
    wait(gv_group.at[0], send_sem.at[GV_OWN])
    wait(gv_group.at[0 : NX - 1], send_sem.at[GV_C])
    wait(part_send.at[0 : NY - 1], send_sem.at[PART])
    wait(fin_send.at[0:15], send_sem.at[FIN])

    @pl.when(jnp.logical_not(gives_own))
    def _():
        wait(fin_send.at[0], send_sem.at[FIN])


def shards(tokens, queries, keys, grad_attended, w_value):
    total_tokens = lax.axis_size("node") * lax.axis_size("local") * tokens.shape[0]
    loss_scale = float(total_tokens) ** -0.5

    def body(*refs):
        kernel(*refs, loss_scale=loss_scale)

    return pl.pallas_call(
        body,
        out_shape=(
            jax.ShapeDtypeStruct((ROWS, KW), BF16),
            jax.ShapeDtypeStruct((4, KW), F32),
        ),
        in_specs=[pl.BlockSpec(memory_space=pl.ANY)] * 5,
        out_specs=(pl.BlockSpec(memory_space=pltpu.VMEM),) * 2,
        scratch_shapes=[
            pltpu.VMEM((ROWS, 4096), BF16),
            pltpu.VMEM((ROWS, 4096), BF16),
            pltpu.VMEM((ROWS, KW), BF16),
            pltpu.VMEM((ROWS, 4096), BF16),
            pltpu.VMEM((1024, KW), BF16),
            pltpu.VMEM((64, NZH - 1, 16, KW), BF16),
            pltpu.VMEM((KVH, GROUP * ROWS, ROWS), BF16),
            pltpu.VMEM((NG, ROWS, KW), BF16),
            pltpu.VMEM((NG, ROWS, KW), BF16),
            pltpu.VMEM((NY, NZH, 16, KW), BF16),
            pltpu.VMEM((NY, NZH, 16, KW), BF16),
            pltpu.VMEM((16, 4, KW), F32),
            pltpu.VMEM((16, 4, KW), F32),
            pltpu.SemaphoreType.DMA((5,)),
            pltpu.SemaphoreType.DMA((10,)),
            pltpu.SemaphoreType.DMA((10,)),
        ],
        compiler_params=pltpu.CompilerParams(
            collective_id=0, has_side_effects=True, vmem_limit_bytes=48 * 1024 * 1024
        ),
        cost_estimate=pl.CostEstimate(
            flops=1_700_000_000, bytes_accessed=5_000_000, transcendentals=524_288
        ),
    )(tokens, queries, keys, grad_attended, w_value)


def solution(mesh):
    in_specs = (
        P(("node", "local"), None),
        P(("node", "local"), None),
        P(("node", "local"), None),
        P(("node", "local"), None),
        P("local", None),
    )
    out_specs = (P(("node", "local"), None), P(("local", "node"), None))
    return jax.shard_map(shards, mesh=mesh, in_specs=in_specs, out_specs=out_specs, check_vma=False)
```

```python
import jax
import jax.numpy as jnp
from jax import lax
from jax.experimental import pallas as pl
from jax.experimental.pallas import tpu as pltpu
from jax.sharding import PartitionSpec as P

HD = 128
KVH = 4
GROUP = 8
ROWS = 128
KW = 512
NX, NY, NZL, NZH, NC = 4, 8, 4, 4, 2
NG = NX * NC
W_Z, W_Y, GV_X, GV_OWN, GV_C, PAIR, VAL, FIN, TOK, PART = 0, 1, 2, 3, 4, 5, 6, 7, 8, 12
MESH = pl.DeviceIdType.MESH
F32 = jnp.float32
BF16 = jnp.bfloat16


def node_of(y, x, z_lo, core):
    return ((y * NX + x) * NZL + z_lo) * NC + core


def over_rows(left, right):
    return lax.dot_general(left, right, (((0,), (0,)), ((), ())), preferred_element_type=F32)


def over_columns(left, right):
    return lax.dot_general(left, right, (((1,), (1,)), ((), ())), preferred_element_type=F32)


def stacked(ref, a):
    return jnp.concatenate(
        [ref[:, (a * GROUP + g) * HD : (a * GROUP + g + 1) * HD] for g in range(GROUP)], axis=0
    )


def kernel(
    tok_hbm, q_hbm, k_hbm, g_hbm, w_hbm, dk_ref, gw_ref,
    q, k, g, w_far, w_cat, soft, tok_group, gv_group, part_send, part_recv,
    fin_send, fin_recv, pair_send, pair_recv, val_send, val_recv,
    load_sem, send_sem, recv_sem, *, loss_scale,
):
    node, z_hi = lax.axis_index("node"), lax.axis_index("local")
    core = lax.rem(node, NC)
    z_lo = lax.rem(node // NC, NZL)
    x = lax.rem(node // (NC * NZL), NX)
    y = node // (NC * NZL * NX)
    z = z_hi * NZL + z_lo
    p = x * NC + core
    head_scale = float(HD) ** -0.5

    def device(y_, x_, core_):
        return (node_of(y_, x_, z_lo, core_), z_hi)

    sibling = device(y, x, 1 - core)
    x_peers = [lax.rem(x + d, NX) for d in range(1, NX)]
    y_peers = [lax.rem(y + d, NY) for d in range(1, NY)]
    far_peers = [lax.rem(z_hi + d, NZH) for d in range(1, NZH)]

    own_rows = w_hbm.at[pl.ds(pl.multiple_of(p * HD, HD), HD)]
    loads = [
        pltpu.make_async_copy(src, dst, load_sem.at[i])
        for i, (src, dst) in enumerate(
            [(q_hbm, q), (k_hbm, k), (g_hbm, g), (own_rows, w_cat.at[z_hi])]
        )
    ]
    for load in loads:
        load.start()

    barrier = pltpu.get_barrier_semaphore()

    def greet(device_id):
        pl.semaphore_signal(barrier, inc=1, device_id=device_id, device_id_type=MESH)

    giver_y, giver_x, giver_core = x * 2 + z_lo // 2, y // 2, lax.rem(y, 2)
    takes_own = (giver_y == y) & (giver_x == x) & (giver_core == core)
    for z_ in range(NZH * NZL):
        giver = (node_of(giver_y, giver_x, z_ % NZL, giver_core), z_ // NZL)

        @pl.when(jnp.logical_not(takes_own & (z == z_)))
        def _():
            greet(giver)

    for h in far_peers:
        greet((node, h))
    for y_ in y_peers:
        greet(device(y_, x, core))
    for x_ in x_peers:
        for core_ in (core, 1 - core):
            greet(device(y, x_, core_))
    greet(sibling)
    near = 1 + 2 * (NX - 1) + (NY - 1) + (NZH - 1)
    pl.semaphore_wait(barrier, near + NZH * NZL - jnp.where(takes_own, 1, 0))

    def send(src, dst, phase, device_id):
        pltpu.make_async_remote_copy(
            src_ref=src, dst_ref=dst, send_sem=send_sem.at[phase], recv_sem=recv_sem.at[phase],
            device_id=device_id, device_id_type=MESH,
        ).start()

    def wait(ref, sem):
        pltpu.make_async_copy(ref, ref, sem).wait()

    piece = w_hbm.at[pl.ds(pl.multiple_of(p * HD + y * 16, 16), 16)]
    for d, h in enumerate(far_peers):
        send(piece, w_far.at[y, NZH - 2 - d], W_Z, (node, h))

    def columns(zh, p_):
        return tok_hbm.at[:, pl.ds(pl.multiple_of(zh * (NG * HD) + p_ * HD, HD), HD)]

    def swap_tokens(zh):
        for x_ in x_peers:
            for core_ in (core, 1 - core):
                send(
                    columns(zh, x_ * NC + core_), tok_group.at[zh, p], TOK + zh,
                    device(y, x_, core_),
                )
        send(columns(zh, x * NC + 1 - core), tok_group.at[zh, p], TOK + zh, sibling)
        pltpu.make_async_copy(columns(zh, p), tok_group.at[zh, p], recv_sem.at[TOK + zh]).start()

    swap_tokens(0)
    swap_tokens(1)

    row_ids = lax.broadcasted_iota(jnp.int32, (GROUP, ROWS, ROWS), 1).reshape(GROUP * ROWS, ROWS)
    col_ids = lax.broadcasted_iota(jnp.int32, (GROUP * ROWS, ROWS), 1)
    allowed = col_ids <= row_ids

    def softmax_head(a):
        cols = slice(a * HD, (a + 1) * HD)
        scores = over_columns(stacked(q, a), k[:, cols]) * head_scale
        scores = jnp.where(allowed, scores, F32(-1e30))
        raised = jnp.exp(scores - jnp.max(scores, axis=-1, keepdims=True))
        weights = (raised / jnp.sum(raised, axis=-1, keepdims=True)).astype(BF16)
        soft[a] = weights
        gv_group[p, :, cols] = over_rows(weights, stacked(g, a)).astype(BF16)

    for load in loads[:3]:
        load.wait()
    softmax_head(0)
    softmax_head(1)
    wait(w_far.at[0], recv_sem.at[W_Z])
    for y_ in y_peers:
        send(w_far.at[y], w_far.at[y], W_Y, device(y_, x, core))
    softmax_head(2)
    softmax_head(3)

    for x_ in x_peers:
        send(gv_group.at[p], gv_group.at[p], GV_X, device(y, x_, core))
    send(gv_group.at[p], gv_group.at[p], GV_OWN, sibling)
    swap_tokens(2)
    swap_tokens(3)
    wait(gv_group.at[0 : NX - 1], recv_sem.at[GV_X])
    for x_ in x_peers:
        send(gv_group.at[x_ * NC + core], gv_group.at[x_ * NC + core], GV_C, sibling)
    wait(gv_group.at[0], recv_sem.at[GV_OWN])
    wait(gv_group.at[0 : NX - 1], recv_sem.at[GV_C])

    gv_all = gv_group[...].reshape(NG * ROWS, KW)
    for zh in range(NZH):
        wait(tok_group.at[zh], recv_sem.at[TOK + zh])
        term = over_rows(tok_group[zh].reshape(NG * ROWS, HD), gv_all) * loss_scale
        part_send[zh] = term.astype(BF16).reshape(NY, 16, KW)
        for y_ in y_peers:
            send(part_send.at[zh, y_], part_recv.at[zh, y], PART + zh, device(y_, x, core))
        pltpu.make_async_copy(
            part_send.at[zh, y], part_recv.at[zh, y], recv_sem.at[PART + zh]
        ).start()

    wait(w_far.at[0 : NY - 1], recv_sem.at[W_Y])
    loads[3].wait()
    for d, h in enumerate(far_peers):
        w_cat[h] = w_far[:, d].reshape(HD, KW)

    def partial_values(core_):
        total = None
        for zh in range(NZH):
            left = jnp.concatenate([tok_group[zh, x_ * NC + core_] for x_ in range(NX)], axis=0)
            product = jnp.dot(left, w_cat[zh], preferred_element_type=F32)
            total = product if total is None else total + product
        return total.reshape(NX, ROWS, KW)

    pair_send[...] = partial_values(1 - core).astype(BF16)
    send(pair_send, pair_recv, PAIR, sibling)
    val_send[...] = partial_values(core)

    gives_own = (lax.rem(y, 2) == z_lo // 2) & (y // 2 == x) & (x * NC + core == y)

    def finish(zh):
        wait(part_recv.at[zh], recv_sem.at[PART + zh])
        part = part_recv[zh, 0].astype(F32)
        for y_ in range(1, NY):
            part = part + part_recv[zh, y_].astype(F32)
        for i in range(4):
            j = zh * 4 + i
            rows = part[4 * i : 4 * i + 4]
            fin_send[j] = jnp.concatenate(
                [rows[:, c * HD : (c + 1) * HD] for c in range(KW // HD)], axis=0
            ).astype(BF16)
            z_lo_, core_ = lax.rem(y, 2) * 2 + i // 2, i % 2
            owner = (node_of(x * NC + core, y // 2, z_lo_, core_), zh)
            own = gives_own & (z_hi == zh) & (z_lo == z_lo_) & (core == core_)

            @pl.when(own)
            def _():
                pltpu.make_async_copy(fin_send.at[j], fin_recv.at[z], recv_sem.at[FIN]).start()

            @pl.when(jnp.logical_not(own))
            def _():
                send(fin_send.at[j], fin_recv.at[z], FIN, owner)

    finish(0)
    wait(pair_recv, recv_sem.at[PAIR])
    for x_ in range(NX):
        summed = val_send[x_] + pair_recv[x_].astype(F32)
        val_send[x_] = summed
        val_out = summed.astype(BF16)
        pair_recv[x_] = val_out
    for x_ in x_peers:
        send(pair_recv.at[x_], val_recv.at[x], VAL, device(y, x_, core))
    finish(1)
    finish(2)
    finish(3)

    wait(val_recv.at[0 : NX - 1], recv_sem.at[VAL])
    total = val_send[x]
    for x_ in x_peers:
        total = total + val_recv[x_].astype(F32)
    values = total.astype(BF16)
    for a in range(KVH):
        cols = slice(a * HD, (a + 1) * HD)
        grad_probs = over_columns(stacked(g, a), values[:, cols])
        soft_float = soft[a].astype(F32)
        delta = jnp.sum(soft_float * grad_probs, axis=-1, keepdims=True)
        grad_scores = (soft_float * (grad_probs - delta)).astype(BF16)
        dk_ref[:, cols] = (over_rows(grad_scores, stacked(q, a)) * head_scale).astype(BF16)

    wait(fin_recv, recv_sem.at[FIN])
    out = fin_recv[0].astype(F32)
    for z_ in range(1, NZH * NZL):
        out = out + fin_recv[z_].astype(F32)
    for c in range(KW // HD):
        gw_ref[:, c * HD : (c + 1) * HD] = out[4 * c : 4 * c + 4]

    wait(w_far.at[0], send_sem.at[W_Z])
    wait(w_far.at[0 : NY - 1], send_sem.at[W_Y])
    for zh in range(NZH):
        wait(tok_group.at[zh, 0 : NG - 1], send_sem.at[TOK + zh])
        wait(part_send.at[zh, 0 : NY - 1], send_sem.at[PART + zh])
    wait(gv_group.at[0 : NX - 1], send_sem.at[GV_X])
    wait(gv_group.at[0], send_sem.at[GV_OWN])
    wait(gv_group.at[0 : NX - 1], send_sem.at[GV_C])
    wait(pair_send, send_sem.at[PAIR])
    wait(val_recv.at[0 : NX - 1], send_sem.at[VAL])
    wait(fin_send.at[0:15], send_sem.at[FIN])

    @pl.when(jnp.logical_not(gives_own))
    def _():
        wait(fin_send.at[0], send_sem.at[FIN])


def shards(tokens, queries, keys, grad_attended, w_value):
    total_tokens = lax.axis_size("node") * lax.axis_size("local") * tokens.shape[0]
    loss_scale = float(total_tokens) ** -0.5

    def body(*refs):
        kernel(*refs, loss_scale=loss_scale)

    return pl.pallas_call(
        body,
        out_shape=(
            jax.ShapeDtypeStruct((ROWS, KW), BF16),
            jax.ShapeDtypeStruct((4, KW), F32),
        ),
        in_specs=[pl.BlockSpec(memory_space=pl.ANY)] * 5,
        out_specs=(pl.BlockSpec(memory_space=pltpu.VMEM),) * 2,
        scratch_shapes=[
            pltpu.VMEM((ROWS, 4096), BF16),
            pltpu.VMEM((ROWS, KW), BF16),
            pltpu.VMEM((ROWS, 4096), BF16),
            pltpu.VMEM((NY, NZH - 1, 16, KW), BF16),
            pltpu.VMEM((NZH, HD, KW), BF16),
            pltpu.VMEM((KVH, GROUP * ROWS, ROWS), BF16),
            pltpu.VMEM((NZH, NG, ROWS, HD), BF16),
            pltpu.VMEM((NG, ROWS, KW), BF16),
            pltpu.VMEM((NZH, NY, 16, KW), BF16),
            pltpu.VMEM((NZH, NY, 16, KW), BF16),
            pltpu.VMEM((16, 16, HD), BF16),
            pltpu.VMEM((16, 16, HD), BF16),
            pltpu.VMEM((NX, ROWS, KW), BF16),
            pltpu.VMEM((NX, ROWS, KW), BF16),
            pltpu.VMEM((NX, ROWS, KW), F32),
            pltpu.VMEM((NX, ROWS, KW), BF16),
            pltpu.SemaphoreType.DMA((4,)),
            pltpu.SemaphoreType.DMA((16,)),
            pltpu.SemaphoreType.DMA((16,)),
        ],
        compiler_params=pltpu.CompilerParams(
            collective_id=0, has_side_effects=True, vmem_limit_bytes=60 * 1024 * 1024
        ),
        cost_estimate=pl.CostEstimate(
            flops=1_700_000_000, bytes_accessed=5_000_000, transcendentals=524_288
        ),
    )(tokens, queries, keys, grad_attended, w_value)


def solution(mesh):
    in_specs = (
        P(("node", "local"), None),
        P(("node", "local"), None),
        P(("node", "local"), None),
        P(("node", "local"), None),
        P("local", None),
    )
    out_specs = (P(("node", "local"), None), P(("local", "node"), None))
    return jax.shard_map(shards, mesh=mesh, in_specs=in_specs, out_specs=out_specs, check_vma=False)
```

```python
import jax
import jax.numpy as jnp
from jax import lax
from jax.experimental import pallas as pl
from jax.experimental.pallas import tpu as pltpu
from jax.sharding import PartitionSpec as P

HD = 128
KVH = 4
GROUP = 8
ROWS = 128
KW = 512
NX, NY, NZL, NZH, NC = 4, 8, 4, 4, 2
NG = NX * NC
W_Z, W_Y, FIN, GV_X, GV_OWN, GV_C, VAL, TOK, PART, PAIR = 0, 1, 2, 3, 5, 7, 9, 11, 15, 19
LOG2_E = 1.4426950408889634
MESH = pl.DeviceIdType.MESH
F32 = jnp.float32
BF16 = jnp.bfloat16


def node_of(y, x, z_lo, core):
    return ((y * NX + x) * NZL + z_lo) * NC + core


def over_columns(left, right):
    return lax.dot_general(left, right, (((1,), (1,)), ((), ())), preferred_element_type=F32)


def stacked(ref, a):
    return jnp.concatenate(
        [ref[:, (a * GROUP + g) * HD : (a * GROUP + g + 1) * HD] for g in range(GROUP)], axis=0
    )


def kernel(
    tok_hbm, q_hbm, k_hbm, g_hbm, w_hbm, dk_ref, gw_ref,
    q, k, g, w_far, w_cat, soft, tok_group, tok_turned, gv_group, part_send, part_recv,
    fin_send, fin_recv, pair_send, pair_recv, val_own, val_other, val_send, val_recv,
    load_sem, send_sem, recv_sem, *, loss_scale,
):
    node, z_hi = lax.axis_index("node"), lax.axis_index("local")
    core = lax.rem(node, NC)
    z_lo = lax.rem(node // NC, NZL)
    x = lax.rem(node // (NC * NZL), NX)
    y = node // (NC * NZL * NX)
    z = z_hi * NZL + z_lo
    p = x * NC + core
    head_scale = float(HD) ** -0.5

    def device(y_, x_, core_):
        return (node_of(y_, x_, z_lo, core_), z_hi)

    sibling = device(y, x, 1 - core)
    x_peers = [lax.rem(x + d, NX) for d in range(1, NX)]
    y_peers = [lax.rem(y + d, NY) for d in range(1, NY)]
    far_peers = [lax.rem(z_hi + d, NZH) for d in range(1, NZH)]

    own_rows = w_hbm.at[pl.ds(pl.multiple_of(p * HD, HD), HD)]
    loads = [
        pltpu.make_async_copy(src, dst, load_sem.at[i])
        for i, (src, dst) in enumerate(
            [(q_hbm, q), (k_hbm, k), (g_hbm, g), (own_rows, w_cat.at[z_hi])]
        )
    ]
    for load in loads:
        load.start()

    barrier = pltpu.get_barrier_semaphore()

    def greet(device_id):
        pl.semaphore_signal(barrier, inc=1, device_id=device_id, device_id_type=MESH)

    giver_y, giver_x, giver_core = x * 2 + z_lo // 2, y // 2, lax.rem(y, 2)
    takes_own = (giver_y == y) & (giver_x == x) & (giver_core == core)
    for z_ in range(NZH * NZL):
        giver = (node_of(giver_y, giver_x, z_ % NZL, giver_core), z_ // NZL)

        @pl.when(jnp.logical_not(takes_own & (z == z_)))
        def _():
            greet(giver)

    for h in far_peers:
        greet((node, h))
    for y_ in y_peers:
        greet(device(y_, x, core))
    for x_ in x_peers:
        for core_ in (core, 1 - core):
            greet(device(y, x_, core_))
    greet(sibling)
    near = 1 + 2 * (NX - 1) + (NY - 1) + (NZH - 1)
    pl.semaphore_wait(barrier, near + NZH * NZL - jnp.where(takes_own, 1, 0))

    def send(src, dst, phase, device_id):
        pltpu.make_async_remote_copy(
            src_ref=src, dst_ref=dst, send_sem=send_sem.at[phase], recv_sem=recv_sem.at[phase],
            device_id=device_id, device_id_type=MESH,
        ).start()

    def wait(ref, sem):
        pltpu.make_async_copy(ref, ref, sem).wait()

    piece = w_hbm.at[pl.ds(pl.multiple_of(p * HD + y * 16, 16), 16)]
    for d, h in enumerate(far_peers):
        send(piece, w_far.at[y, NZH - 2 - d], W_Z, (node, h))

    def columns(zh, p_):
        return tok_hbm.at[:, pl.ds(pl.multiple_of(zh * (NG * HD) + p_ * HD, HD), HD)]

    def place(zh):
        return tok_group.at[zh // 2, p, :, (zh % 2) * HD : (zh % 2 + 1) * HD]

    def swap_tokens(zh):
        for x_ in x_peers:
            for core_ in (core, 1 - core):
                send(columns(zh, x_ * NC + core_), place(zh), TOK + zh, device(y, x_, core_))
        send(columns(zh, x * NC + 1 - core), place(zh), TOK + zh, sibling)
        pltpu.make_async_copy(columns(zh, p), place(zh), recv_sem.at[TOK + zh]).start()

    swap_tokens(0)

    key_ids = lax.broadcasted_iota(jnp.int32, (ROWS, 2 * ROWS), 0)
    lane_ids = lax.broadcasted_iota(jnp.int32, (ROWS, 2 * ROWS), 1)
    allowed = key_ids <= lax.rem(lane_ids, ROWS)
    exponent_scale = head_scale * LOG2_E

    def heads(ref, a, pair):
        first = a * GROUP + 2 * pair
        return jnp.concatenate(
            [ref[:, h * HD : (h + 1) * HD] for h in (first, first + 1)], axis=0
        )

    def softmax_head(a):
        cols = slice(a * HD, (a + 1) * HD)
        keys_a = k[:, cols]
        for pair in range(GROUP // 2):
            scores = over_columns(keys_a, heads(q, a, pair))
            scores = jnp.where(allowed, scores, F32(-1e30))
            peak = jnp.max(scores, axis=0, keepdims=True)
            raised = jnp.exp2((scores - peak) * exponent_scale)
            inverse = 1.0 / jnp.sum(raised, axis=0, keepdims=True)
            soft[a, :, pair * 2 * ROWS : (pair + 1) * 2 * ROWS] = (raised * inverse).astype(BF16)
        gv_group[a // 2, p, :, (a % 2) * HD : (a % 2 + 1) * HD] = jnp.dot(
            soft[a], stacked(g, a), preferred_element_type=F32
        ).astype(BF16)

    def share_grads(half):
        mine = gv_group.at[half, p]
        for x_ in x_peers:
            send(mine, mine, GV_X + half, device(y, x_, core))
        send(mine, mine, GV_OWN + half, sibling)

    def pass_grads(half):
        wait(gv_group.at[half, 0 : NX - 1], recv_sem.at[GV_X + half])
        for x_ in x_peers:
            theirs = gv_group.at[half, x_ * NC + core]
            send(theirs, theirs, GV_C + half, sibling)

    def turn_tokens(zh):
        wait(tok_group.at[0, 0 : NG // 2], recv_sem.at[TOK + zh])
        lanes = slice((zh % 2) * HD, (zh % 2 + 1) * HD)
        tok_turned[zh] = tok_group[zh // 2, :, :, lanes].reshape(NG * ROWS, HD).T

    for load in loads[:3]:
        load.wait()
    softmax_head(0)
    softmax_head(1)
    share_grads(0)
    softmax_head(2)
    softmax_head(3)
    share_grads(1)
    wait(w_far.at[0], recv_sem.at[W_Z])
    for y_ in y_peers:
        send(w_far.at[y], w_far.at[y], W_Y, device(y_, x, core))
    turn_tokens(0)
    pass_grads(0)
    swap_tokens(1)
    pass_grads(1)
    swap_tokens(2)
    swap_tokens(3)
    for half in range(2):
        wait(gv_group.at[half, 0], recv_sem.at[GV_OWN + half])
        wait(gv_group.at[half, 0 : NX - 1], recv_sem.at[GV_C + half])

    def term_rows(zh):
        for half in range(2):
            term = jnp.dot(
                tok_turned[zh], gv_group[half].reshape(NG * ROWS, KW // 2),
                preferred_element_type=F32,
            )
            term = (term * loss_scale).astype(BF16).reshape(NY, 16, KW // 2)
            part_send[zh, :, :, half * (KW // 2) : (half + 1) * (KW // 2)] = term
        for y_ in y_peers:
            send(part_send.at[zh, y_], part_recv.at[zh, y], PART + zh, device(y_, x, core))
        pltpu.make_async_copy(
            part_send.at[zh, y], part_recv.at[zh, y], recv_sem.at[PART + zh]
        ).start()

    def partial_values(pair, core_):
        left = jnp.concatenate([tok_group[pair, x_ * NC + core_] for x_ in range(NX)], axis=0)
        right = w_cat[2 * pair : 2 * pair + 2].reshape(2 * HD, KW)
        product = jnp.dot(left, right, preferred_element_type=F32)
        return product.reshape(NX, ROWS, KW)

    gives_own = (lax.rem(y, 2) == z_lo // 2) & (y // 2 == x) & (x * NC + core == y)

    def finish(zh):
        wait(part_recv.at[zh], recv_sem.at[PART + zh])
        part = part_recv[zh, 0].astype(F32)
        for y_ in range(1, NY):
            part = part + part_recv[zh, y_].astype(F32)
        for i in range(4):
            j = zh * 4 + i
            rows = part[4 * i : 4 * i + 4]
            fin_send[j] = jnp.concatenate(
                [rows[:, c * HD : (c + 1) * HD] for c in range(KW // HD)], axis=0
            ).astype(BF16)
            z_lo_, core_ = lax.rem(y, 2) * 2 + i // 2, i % 2
            owner = (node_of(x * NC + core, y // 2, z_lo_, core_), zh)
            own = gives_own & (z_hi == zh) & (z_lo == z_lo_) & (core == core_)

            @pl.when(own)
            def _():
                pltpu.make_async_copy(fin_send.at[j], fin_recv.at[z], recv_sem.at[FIN]).start()

            @pl.when(jnp.logical_not(own))
            def _():
                send(fin_send.at[j], fin_recv.at[z], FIN, owner)

    term_rows(0)
    wait(w_far.at[0 : NY - 1], recv_sem.at[W_Y])
    loads[3].wait()
    for d, h in enumerate(far_peers):
        w_cat[h] = w_far[:, d].reshape(HD, KW)
    turn_tokens(1)
    term_rows(1)
    val_other[...] = partial_values(0, 1 - core)
    val_own[...] = partial_values(0, core)
    turn_tokens(2)
    term_rows(2)
    finish(0)
    turn_tokens(3)
    term_rows(3)
    pair_send[...] = (val_other[...] + partial_values(1, 1 - core)).astype(BF16)
    for i, x_ in enumerate(x_peers + [x]):
        send(pair_send.at[x_], pair_recv.at[x_], PAIR + i, sibling)
    val_own[...] = val_own[...] + partial_values(1, core)

    for i, x_ in enumerate(x_peers):
        wait(pair_recv.at[x_], recv_sem.at[PAIR + i])
        val_send[x_] = (val_own[x_] + pair_recv[x_].astype(F32)).astype(BF16)
        for half in range(2):
            lanes = slice(half * (KW // 2), (half + 1) * (KW // 2))
            send(
                val_send.at[x_, :, lanes], val_recv.at[half, x], VAL + half, device(y, x_, core)
            )
    finish(1)
    finish(2)
    finish(3)

    wait(pair_recv.at[x], recv_sem.at[PAIR + NX - 1])
    for half in range(2):
        lanes = slice(half * (KW // 2), (half + 1) * (KW // 2))
        total = val_own[x, :, lanes] + pair_recv[x, :, lanes].astype(F32)
        wait(val_recv.at[half, 0 : NX - 1], recv_sem.at[VAL + half])
        for x_ in x_peers:
            total = total + val_recv[half, x_].astype(F32)
        values = total.astype(BF16)
        for a in (2 * half, 2 * half + 1):
            values_a = values[:, (a % 2) * HD : (a % 2 + 1) * HD]
            grad_scores = []
            for pair in range(GROUP // 2):
                grad_probs = over_columns(values_a, heads(g, a, pair))
                soft_float = soft[a, :, pair * 2 * ROWS : (pair + 1) * 2 * ROWS].astype(F32)
                delta = jnp.sum(soft_float * grad_probs, axis=0, keepdims=True)
                grad_scores.append((soft_float * (grad_probs - delta)).astype(BF16))
            d_keys = jnp.dot(
                jnp.concatenate(grad_scores, axis=1), stacked(q, a), preferred_element_type=F32
            )
            dk_ref[:, a * HD : (a + 1) * HD] = (d_keys * head_scale).astype(BF16)

    wait(fin_recv, recv_sem.at[FIN])
    out = fin_recv[0].astype(F32)
    for z_ in range(1, NZH * NZL):
        out = out + fin_recv[z_].astype(F32)
    for c in range(KW // HD):
        gw_ref[:, c * HD : (c + 1) * HD] = out[4 * c : 4 * c + 4]

    wait(w_far.at[0], send_sem.at[W_Z])
    wait(w_far.at[0 : NY - 1], send_sem.at[W_Y])
    for zh in range(NZH):
        wait(gv_group.at[0, 0:7, :, 0:128], send_sem.at[TOK + zh])
        wait(part_send.at[zh, 0 : NY - 1], send_sem.at[PART + zh])
    for half in range(2):
        wait(gv_group.at[half, 0 : NX - 1], send_sem.at[GV_X + half])
        wait(gv_group.at[half, 0], send_sem.at[GV_OWN + half])
        wait(gv_group.at[half, 0 : NX - 1], send_sem.at[GV_C + half])
        wait(val_recv.at[half, 0 : NX - 1], send_sem.at[VAL + half])
    for i in range(NX):
        wait(pair_send.at[0], send_sem.at[PAIR + i])
    wait(fin_send.at[0:15], send_sem.at[FIN])

    @pl.when(jnp.logical_not(gives_own))
    def _():
        wait(fin_send.at[0], send_sem.at[FIN])


def shards(tokens, queries, keys, grad_attended, w_value):
    total_tokens = lax.axis_size("node") * lax.axis_size("local") * tokens.shape[0]
    loss_scale = float(total_tokens) ** -0.5

    def body(*refs):
        kernel(*refs, loss_scale=loss_scale)

    return pl.pallas_call(
        body,
        out_shape=(
            pltpu.VMEM((ROWS, KW), BF16),
            pltpu.VMEM((4, KW), F32),
        ),
        in_specs=[pl.BlockSpec(memory_space=pl.ANY)] * 5,
        out_specs=(pl.BlockSpec(memory_space=pltpu.VMEM),) * 2,
        scratch_shapes=[
            pltpu.VMEM((ROWS, 4096), BF16),
            pltpu.VMEM((ROWS, KW), BF16),
            pltpu.VMEM((ROWS, 4096), BF16),
            pltpu.VMEM((NY, NZH - 1, 16, KW), BF16),
            pltpu.VMEM((NZH, HD, KW), BF16),
            pltpu.VMEM((KVH, ROWS, GROUP * ROWS), BF16),
            pltpu.VMEM((2, NG, ROWS, 2 * HD), BF16),
            pltpu.VMEM((NZH, HD, NG * ROWS), BF16),
            pltpu.VMEM((2, NG, ROWS, KW // 2), BF16),
            pltpu.VMEM((NZH, NY, 16, KW), BF16),
            pltpu.VMEM((NZH, NY, 16, KW), BF16),
            pltpu.VMEM((16, 16, HD), BF16),
            pltpu.VMEM((16, 16, HD), BF16),
            pltpu.VMEM((NX, ROWS, KW), BF16),
            pltpu.VMEM((NX, ROWS, KW), BF16),
            pltpu.VMEM((NX, ROWS, KW), F32),
            pltpu.VMEM((NX, ROWS, KW), F32),
            pltpu.VMEM((NX, ROWS, KW), BF16),
            pltpu.VMEM((2, NX, ROWS, KW // 2), BF16),
            pltpu.SemaphoreType.DMA((4,)),
            pltpu.SemaphoreType.DMA((23,)),
            pltpu.SemaphoreType.DMA((23,)),
        ],
        compiler_params=pltpu.CompilerParams(
            collective_id=0, has_side_effects=True, vmem_limit_bytes=60 * 1024 * 1024
        ),
        cost_estimate=pl.CostEstimate(
            flops=1_700_000_000, bytes_accessed=5_000_000, transcendentals=524_288
        ),
    )(tokens, queries, keys, grad_attended, w_value)


def solution(mesh):
    in_specs = (
        P(("node", "local"), None),
        P(("node", "local"), None),
        P(("node", "local"), None),
        P(("node", "local"), None),
        P("local", None),
    )
    out_specs = (P(("node", "local"), None), P(("local", "node"), None))
    return jax.shard_map(shards, mesh=mesh, in_specs=in_specs, out_specs=out_specs, check_vma=False)
```

```python
import jax
import jax.numpy as jnp
from jax import lax
from jax.experimental import pallas as pl
from jax.experimental.pallas import tpu as pltpu
from jax.sharding import PartitionSpec as P

HD = 128
KVH = 4
GROUP = 8
ROWS = 128
KW = 512
NX, NY, NZL, NZH, NC = 4, 8, 4, 4, 2
NG = NX * NC
W_Z, W_L, FIN, GV_X, GV_OWN, GV_C, VAL, TOK, PART, PAIR = 0, 1, 2, 3, 5, 7, 9, 11, 15, 19
LOG2_E = 1.4426950408889634
MESH = pl.DeviceIdType.MESH
F32 = jnp.float32
BF16 = jnp.bfloat16


def node_of(y, x, z_lo, core):
    return ((y * NX + x) * NZL + z_lo) * NC + core


def over_columns(left, right):
    return lax.dot_general(left, right, (((1,), (1,)), ((), ())), preferred_element_type=F32)


def stacked(ref, a):
    return jnp.concatenate(
        [ref[:, (a * GROUP + g) * HD : (a * GROUP + g + 1) * HD] for g in range(GROUP)], axis=0
    )


def kernel(
    tok_hbm, q_hbm, k_hbm, g_hbm, w_hbm, dk_ref, gw_ref,
    q, k, g, w_far, w_cat, soft, tok_group, tok_turned, gv_group, part_send, part_recv,
    fin_send, fin_recv, pair_send, pair_recv, val_own, val_send, val_recv,
    load_sem, send_sem, recv_sem, *, loss_scale,
):
    node, z_hi = lax.axis_index("node"), lax.axis_index("local")
    core = lax.rem(node, NC)
    z_lo = lax.rem(node // NC, NZL)
    x = lax.rem(node // (NC * NZL), NX)
    y = node // (NC * NZL * NX)
    z = z_hi * NZL + z_lo
    p = x * NC + core
    head_scale = float(HD) ** -0.5

    def device(y_, x_, core_):
        return (node_of(y_, x_, z_lo, core_), z_hi)

    sibling = device(y, x, 1 - core)
    x_peers = [lax.rem(x + d, NX) for d in range(1, NX)]
    y_peers = [lax.rem(y + d, NY) for d in range(1, NY)]
    line_peers = [lax.rem(z_lo + d, NZL) for d in range(1, NZL)]
    far_peers = [lax.rem(z_hi + d, NZH) for d in range(1, NZH)]

    own_rows = w_hbm.at[pl.ds(pl.multiple_of(p * HD, HD), HD)]
    loads = [
        pltpu.make_async_copy(src, dst, load_sem.at[i])
        for i, (src, dst) in enumerate(
            [(q_hbm, q), (k_hbm, k), (g_hbm, g), (own_rows, w_cat.at[z_hi])]
        )
    ]
    for load in loads:
        load.start()

    barrier = pltpu.get_barrier_semaphore()

    def greet(device_id):
        pl.semaphore_signal(barrier, inc=1, device_id=device_id, device_id_type=MESH)

    giver_y, giver_x, giver_core = x * 2 + z_lo // 2, y // 2, lax.rem(y, 2)
    takes_own = (giver_y == y) & (giver_x == x) & (giver_core == core)
    for z_ in range(NZH * NZL):
        giver = (node_of(giver_y, giver_x, z_ % NZL, giver_core), z_ // NZL)

        @pl.when(jnp.logical_not(takes_own & (z == z_)))
        def _():
            greet(giver)

    for h in far_peers:
        greet((node, h))
    for z_lo_ in line_peers:
        greet((node_of(y, x, z_lo_, core), z_hi))
    for y_ in y_peers:
        greet(device(y_, x, core))
    for x_ in x_peers:
        for core_ in (core, 1 - core):
            greet(device(y, x_, core_))
    greet(sibling)
    near = 1 + 2 * (NX - 1) + (NY - 1) + (NZH - 1) + (NZL - 1)
    pl.semaphore_wait(barrier, near + NZH * NZL - jnp.where(takes_own, 1, 0))

    def send(src, dst, phase, device_id):
        pltpu.make_async_remote_copy(
            src_ref=src, dst_ref=dst, send_sem=send_sem.at[phase], recv_sem=recv_sem.at[phase],
            device_id=device_id, device_id_type=MESH,
        ).start()

    def wait(ref, sem):
        pltpu.make_async_copy(ref, ref, sem).wait()

    piece = w_hbm.at[pl.ds(pl.multiple_of(p * HD + z_lo * 32, 32), 32)]
    for d, h in enumerate(far_peers):
        send(piece, w_far.at[z_lo, NZH - 2 - d], W_Z, (node, h))

    def columns(zh, p_):
        return tok_hbm.at[:, pl.ds(pl.multiple_of(zh * (NG * HD) + p_ * HD, HD), HD)]

    def place(zh):
        return tok_group.at[zh // 2, p, :, (zh % 2) * HD : (zh % 2 + 1) * HD]

    def swap_tokens(zh):
        for x_ in x_peers:
            for core_ in (core, 1 - core):
                send(columns(zh, x_ * NC + core_), place(zh), TOK + zh, device(y, x_, core_))
        send(columns(zh, x * NC + 1 - core), place(zh), TOK + zh, sibling)
        pltpu.make_async_copy(columns(zh, p), place(zh), recv_sem.at[TOK + zh]).start()

    swap_tokens(0)

    key_ids = lax.broadcasted_iota(jnp.int32, (ROWS, 2 * ROWS), 0)
    lane_ids = lax.broadcasted_iota(jnp.int32, (ROWS, 2 * ROWS), 1)
    allowed = key_ids <= lax.rem(lane_ids, ROWS)
    exponent_scale = head_scale * LOG2_E

    def heads(ref, a, pair):
        first = a * GROUP + 2 * pair
        return jnp.concatenate(
            [ref[:, h * HD : (h + 1) * HD] for h in (first, first + 1)], axis=0
        )

    def softmax_head(a):
        cols = slice(a * HD, (a + 1) * HD)
        keys_a = k[:, cols]
        for pair in range(GROUP // 2):
            scores = over_columns(keys_a, heads(q, a, pair))
            scores = jnp.where(allowed, scores, F32(-1e30))
            peak = jnp.max(scores, axis=0, keepdims=True)
            raised = jnp.exp2((scores - peak) * exponent_scale)
            inverse = 1.0 / jnp.sum(raised, axis=0, keepdims=True)
            soft[a, :, pair * 2 * ROWS : (pair + 1) * 2 * ROWS] = (raised * inverse).astype(BF16)
        gv_group[a // 2, p, :, (a % 2) * HD : (a % 2 + 1) * HD] = jnp.dot(
            soft[a], stacked(g, a), preferred_element_type=F32
        ).astype(BF16)

    def share_grads(half):
        mine = gv_group.at[half, p]
        for x_ in x_peers:
            send(mine, mine, GV_X + half, device(y, x_, core))
        send(mine, mine, GV_OWN + half, sibling)

    def pass_grads(half):
        wait(gv_group.at[half, 0 : NX - 1], recv_sem.at[GV_X + half])
        for x_ in x_peers:
            theirs = gv_group.at[half, x_ * NC + core]
            send(theirs, theirs, GV_C + half, sibling)

    def turn_tokens(zh):
        wait(tok_group.at[0, 0 : NG // 2], recv_sem.at[TOK + zh])
        lanes = slice((zh % 2) * HD, (zh % 2 + 1) * HD)
        tok_turned[zh] = tok_group[zh // 2, :, :, lanes].reshape(NG * ROWS, HD).T

    for load in loads[:3]:
        load.wait()
    softmax_head(0)
    softmax_head(1)
    share_grads(0)
    softmax_head(2)
    softmax_head(3)
    share_grads(1)
    wait(w_far.at[0], recv_sem.at[W_Z])
    for z_lo_ in line_peers:
        send(w_far.at[z_lo], w_far.at[z_lo], W_L, (node_of(y, x, z_lo_, core), z_hi))
    turn_tokens(0)
    pass_grads(0)
    swap_tokens(1)
    pass_grads(1)
    swap_tokens(2)
    swap_tokens(3)
    for half in range(2):
        wait(gv_group.at[half, 0], recv_sem.at[GV_OWN + half])
        wait(gv_group.at[half, 0 : NX - 1], recv_sem.at[GV_C + half])

    def term_rows(zh):
        for half in range(2):
            term = jnp.dot(
                tok_turned[zh], gv_group[half].reshape(NG * ROWS, KW // 2),
                preferred_element_type=F32,
            )
            term = (term * loss_scale).astype(BF16).reshape(NY, 16, KW // 2)
            part_send[zh, :, :, half * (KW // 2) : (half + 1) * (KW // 2)] = term
        for y_ in y_peers:
            send(part_send.at[zh, y_], part_recv.at[zh, y], PART + zh, device(y_, x, core))
        pltpu.make_async_copy(
            part_send.at[zh, y], part_recv.at[zh, y], recv_sem.at[PART + zh]
        ).start()

    def partial_values(core_):
        total = None
        for pair in range(2):
            left = jnp.concatenate([tok_group[pair, x_ * NC + core_] for x_ in range(NX)], axis=0)
            right = w_cat[2 * pair : 2 * pair + 2].reshape(2 * HD, KW)
            product = jnp.dot(left, right, preferred_element_type=F32)
            total = product if total is None else total + product
        return total.reshape(NX, ROWS, KW)

    gives_own = (lax.rem(y, 2) == z_lo // 2) & (y // 2 == x) & (x * NC + core == y)

    def finish(zh):
        wait(part_recv.at[zh], recv_sem.at[PART + zh])
        part = part_recv[zh, 0].astype(F32)
        for y_ in range(1, NY):
            part = part + part_recv[zh, y_].astype(F32)
        for i in range(4):
            j = zh * 4 + i
            rows = part[4 * i : 4 * i + 4]
            fin_send[j] = jnp.concatenate(
                [rows[:, c * HD : (c + 1) * HD] for c in range(KW // HD)], axis=0
            ).astype(BF16)
            z_lo_, core_ = lax.rem(y, 2) * 2 + i // 2, i % 2
            owner = (node_of(x * NC + core, y // 2, z_lo_, core_), zh)
            own = gives_own & (z_hi == zh) & (z_lo == z_lo_) & (core == core_)

            @pl.when(own)
            def _():
                pltpu.make_async_copy(fin_send.at[j], fin_recv.at[z], recv_sem.at[FIN]).start()

            @pl.when(jnp.logical_not(own))
            def _():
                send(fin_send.at[j], fin_recv.at[z], FIN, owner)

    term_rows(0)
    turn_tokens(1)
    term_rows(1)
    turn_tokens(2)
    term_rows(2)
    finish(0)
    turn_tokens(3)
    term_rows(3)
    wait(w_far.at[0 : NZL - 1], recv_sem.at[W_L])
    loads[3].wait()
    for d, h in enumerate(far_peers):
        w_cat[h] = w_far[:, d].reshape(HD, KW)
    pair_send[...] = partial_values(1 - core).astype(BF16)
    for i, x_ in enumerate(x_peers + [x]):
        send(pair_send.at[x_], pair_recv.at[x_], PAIR + i, sibling)
    val_own[...] = partial_values(core)

    for i, x_ in enumerate(x_peers):
        wait(pair_recv.at[x_], recv_sem.at[PAIR + i])
        val_send[x_] = (val_own[x_] + pair_recv[x_].astype(F32)).astype(BF16)
        for half in range(2):
            lanes = slice(half * (KW // 2), (half + 1) * (KW // 2))
            send(
                val_send.at[x_, :, lanes], val_recv.at[half, x], VAL + half, device(y, x_, core)
            )
    finish(1)
    finish(2)
    finish(3)

    wait(pair_recv.at[x], recv_sem.at[PAIR + NX - 1])
    for half in range(2):
        lanes = slice(half * (KW // 2), (half + 1) * (KW // 2))
        total = val_own[x, :, lanes] + pair_recv[x, :, lanes].astype(F32)
        wait(val_recv.at[half, 0 : NX - 1], recv_sem.at[VAL + half])
        for x_ in x_peers:
            total = total + val_recv[half, x_].astype(F32)
        values = total.astype(BF16)
        for a in (2 * half, 2 * half + 1):
            values_a = values[:, (a % 2) * HD : (a % 2 + 1) * HD]
            grad_scores = []
            for pair in range(GROUP // 2):
                grad_probs = over_columns(values_a, heads(g, a, pair))
                soft_float = soft[a, :, pair * 2 * ROWS : (pair + 1) * 2 * ROWS].astype(F32)
                delta = jnp.sum(soft_float * grad_probs, axis=0, keepdims=True)
                grad_scores.append((soft_float * (grad_probs - delta)).astype(BF16))
            d_keys = jnp.dot(
                jnp.concatenate(grad_scores, axis=1), stacked(q, a), preferred_element_type=F32
            )
            dk_ref[:, a * HD : (a + 1) * HD] = (d_keys * head_scale).astype(BF16)

    wait(fin_recv, recv_sem.at[FIN])
    out = fin_recv[0].astype(F32)
    for z_ in range(1, NZH * NZL):
        out = out + fin_recv[z_].astype(F32)
    for c in range(KW // HD):
        gw_ref[:, c * HD : (c + 1) * HD] = out[4 * c : 4 * c + 4]

    wait(w_far.at[0], send_sem.at[W_Z])
    wait(w_far.at[0 : NZL - 1], send_sem.at[W_L])
    for zh in range(NZH):
        wait(gv_group.at[0, 0:7, :, 0:128], send_sem.at[TOK + zh])
        wait(part_send.at[zh, 0 : NY - 1], send_sem.at[PART + zh])
    for half in range(2):
        wait(gv_group.at[half, 0 : NX - 1], send_sem.at[GV_X + half])
        wait(gv_group.at[half, 0], send_sem.at[GV_OWN + half])
        wait(gv_group.at[half, 0 : NX - 1], send_sem.at[GV_C + half])
        wait(val_recv.at[half, 0 : NX - 1], send_sem.at[VAL + half])
    for i in range(NX):
        wait(pair_send.at[0], send_sem.at[PAIR + i])
    wait(fin_send.at[0:15], send_sem.at[FIN])

    @pl.when(jnp.logical_not(gives_own))
    def _():
        wait(fin_send.at[0], send_sem.at[FIN])


def shards(tokens, queries, keys, grad_attended, w_value):
    total_tokens = lax.axis_size("node") * lax.axis_size("local") * tokens.shape[0]
    loss_scale = float(total_tokens) ** -0.5

    def body(*refs):
        kernel(*refs, loss_scale=loss_scale)

    return pl.pallas_call(
        body,
        out_shape=(
            pltpu.VMEM((ROWS, KW), BF16),
            pltpu.VMEM((4, KW), F32),
        ),
        in_specs=[pl.BlockSpec(memory_space=pl.ANY)] * 5,
        out_specs=(pl.BlockSpec(memory_space=pltpu.VMEM),) * 2,
        scratch_shapes=[
            pltpu.VMEM((ROWS, 4096), BF16),
            pltpu.VMEM((ROWS, KW), BF16),
            pltpu.VMEM((ROWS, 4096), BF16),
            pltpu.VMEM((NZL, NZH - 1, 32, KW), BF16),
            pltpu.VMEM((NZH, HD, KW), BF16),
            pltpu.VMEM((KVH, ROWS, GROUP * ROWS), BF16),
            pltpu.VMEM((2, NG, ROWS, 2 * HD), BF16),
            pltpu.VMEM((NZH, HD, NG * ROWS), BF16),
            pltpu.VMEM((2, NG, ROWS, KW // 2), BF16),
            pltpu.VMEM((NZH, NY, 16, KW), BF16),
            pltpu.VMEM((NZH, NY, 16, KW), BF16),
            pltpu.VMEM((16, 16, HD), BF16),
            pltpu.VMEM((16, 16, HD), BF16),
            pltpu.VMEM((NX, ROWS, KW), BF16),
            pltpu.VMEM((NX, ROWS, KW), BF16),
            pltpu.VMEM((NX, ROWS, KW), F32),
            pltpu.VMEM((NX, ROWS, KW), BF16),
            pltpu.VMEM((2, NX, ROWS, KW // 2), BF16),
            pltpu.SemaphoreType.DMA((4,)),
            pltpu.SemaphoreType.DMA((23,)),
            pltpu.SemaphoreType.DMA((23,)),
        ],
        compiler_params=pltpu.CompilerParams(
            collective_id=0, has_side_effects=True, vmem_limit_bytes=60 * 1024 * 1024
        ),
        cost_estimate=pl.CostEstimate(
            flops=1_700_000_000, bytes_accessed=5_000_000, transcendentals=524_288
        ),
    )(tokens, queries, keys, grad_attended, w_value)


def solution(mesh):
    in_specs = (
        P(("node", "local"), None),
        P(("node", "local"), None),
        P(("node", "local"), None),
        P(("node", "local"), None),
        P("local", None),
    )
    out_specs = (P(("node", "local"), None), P(("local", "node"), None))
    return jax.shard_map(shards, mesh=mesh, in_specs=in_specs, out_specs=out_specs, check_vma=False)
```

```python
import jax
import jax.numpy as jnp
from jax import lax
from jax.experimental import pallas as pl
from jax.experimental.pallas import tpu as pltpu
from jax.sharding import PartitionSpec as P

HD = 128
KVH = 4
GROUP = 8
ROWS = 128
KW = 512
NX, NY, NZL, NZH, NC = 4, 8, 4, 4, 2
NG = NX * NC
W_Z, W_L, FIN, GV_X, GV_OWN, GV_C, VAL, TOK, PART, PAIR = 0, 1, 2, 3, 5, 7, 9, 11, 15, 19
LOG2_E = 1.4426950408889634
MESH = pl.DeviceIdType.MESH
F32 = jnp.float32
BF16 = jnp.bfloat16


def node_of(y, x, z_lo, core):
    return ((y * NX + x) * NZL + z_lo) * NC + core


def over_columns(left, right):
    return lax.dot_general(left, right, (((1,), (1,)), ((), ())), preferred_element_type=F32)


def stacked(ref, a):
    return jnp.concatenate(
        [ref[:, (a * GROUP + g) * HD : (a * GROUP + g + 1) * HD] for g in range(GROUP)], axis=0
    )


def kernel(
    tok_hbm, q_hbm, k_hbm, g_hbm, w_hbm, dk_ref, gw_ref,
    q, k, g, w_far, w_cat, soft, tok_group, tok_turned, gv_group, part_send, part_recv,
    fin_send, fin_recv, pair_send, pair_recv, val_own, val_send, val_recv,
    load_sem, send_sem, recv_sem, *, loss_scale,
):
    node, z_hi = lax.axis_index("node"), lax.axis_index("local")
    core = lax.rem(node, NC)
    z_lo = lax.rem(node // NC, NZL)
    x = lax.rem(node // (NC * NZL), NX)
    y = node // (NC * NZL * NX)
    z = z_hi * NZL + z_lo
    p = x * NC + core
    head_scale = float(HD) ** -0.5

    def device(y_, x_, core_):
        return (node_of(y_, x_, z_lo, core_), z_hi)

    sibling = device(y, x, 1 - core)
    x_peers = [lax.rem(x + d, NX) for d in range(1, NX)]
    y_peers = [lax.rem(y + d, NY) for d in range(1, NY)]
    line_peers = [lax.rem(z_lo + d, NZL) for d in range(1, NZL)]
    far_peers = [lax.rem(z_hi + d, NZH) for d in range(1, NZH)]

    own_rows = w_hbm.at[pl.ds(pl.multiple_of(p * HD, HD), HD)]
    loads = [
        pltpu.make_async_copy(src, dst, load_sem.at[i])
        for i, (src, dst) in enumerate(
            [(q_hbm, q), (k_hbm, k), (g_hbm, g), (own_rows, w_cat.at[z_hi])]
        )
    ]
    for load in loads:
        load.start()

    barrier = pltpu.get_barrier_semaphore()

    def greet(device_id):
        pl.semaphore_signal(barrier, inc=1, device_id=device_id, device_id_type=MESH)

    giver_y, giver_x, giver_core = x * 2 + z_lo // 2, y // 2, lax.rem(y, 2)
    takes_own = (giver_y == y) & (giver_x == x) & (giver_core == core)
    for z_ in range(NZH * NZL):
        giver = (node_of(giver_y, giver_x, z_ % NZL, giver_core), z_ // NZL)

        @pl.when(jnp.logical_not(takes_own & (z == z_)))
        def _():
            greet(giver)

    for h in far_peers:
        greet((node, h))
    for z_lo_ in line_peers:
        greet((node_of(y, x, z_lo_, core), z_hi))
    for y_ in y_peers:
        greet(device(y_, x, core))
    for x_ in x_peers:
        for core_ in (core, 1 - core):
            greet(device(y, x_, core_))
    greet(sibling)
    near = 1 + 2 * (NX - 1) + (NY - 1) + (NZH - 1) + (NZL - 1)
    pl.semaphore_wait(barrier, near + NZH * NZL - jnp.where(takes_own, 1, 0))

    def send(src, dst, phase, device_id):
        pltpu.make_async_remote_copy(
            src_ref=src, dst_ref=dst, send_sem=send_sem.at[phase], recv_sem=recv_sem.at[phase],
            device_id=device_id, device_id_type=MESH,
        ).start()

    def wait(ref, sem):
        pltpu.make_async_copy(ref, ref, sem).wait()

    piece = w_hbm.at[pl.ds(pl.multiple_of(p * HD + z_lo * 32, 32), 32)]
    for d, h in enumerate(far_peers):
        send(piece, w_far.at[z_lo, NZH - 2 - d], W_Z, (node, h))

    def columns(zh, p_):
        return tok_hbm.at[:, pl.ds(pl.multiple_of(zh * (NG * HD) + p_ * HD, HD), HD)]

    def place(zh):
        return tok_group.at[zh // 2, p, :, (zh % 2) * HD : (zh % 2 + 1) * HD]

    def swap_tokens(zh):
        for x_ in x_peers:
            for core_ in (core, 1 - core):
                send(columns(zh, x_ * NC + core_), place(zh), TOK + zh, device(y, x_, core_))
        send(columns(zh, x * NC + 1 - core), place(zh), TOK + zh, sibling)
        pltpu.make_async_copy(columns(zh, p), place(zh), recv_sem.at[TOK + zh]).start()

    swap_tokens(0)

    key_ids = lax.broadcasted_iota(jnp.int32, (ROWS, 2 * ROWS), 0)
    lane_ids = lax.broadcasted_iota(jnp.int32, (ROWS, 2 * ROWS), 1)
    allowed = key_ids <= lax.rem(lane_ids, ROWS)
    exponent_scale = head_scale * LOG2_E

    def heads(ref, a, pair):
        first = a * GROUP + 2 * pair
        return jnp.concatenate(
            [ref[:, h * HD : (h + 1) * HD] for h in (first, first + 1)], axis=0
        )

    def softmax_head(a):
        cols = slice(a * HD, (a + 1) * HD)
        keys_a = k[:, cols]
        for pair in range(GROUP // 2):
            scores = over_columns(keys_a, heads(q, a, pair))
            scores = jnp.where(allowed, scores, F32(-1e30))
            peak = jnp.max(scores, axis=0, keepdims=True)
            raised = jnp.exp2((scores - peak) * exponent_scale)
            inverse = 1.0 / jnp.sum(raised, axis=0, keepdims=True)
            soft[a, :, pair * 2 * ROWS : (pair + 1) * 2 * ROWS] = (raised * inverse).astype(BF16)
        gv_group[a // 2, p, :, (a % 2) * HD : (a % 2 + 1) * HD] = jnp.dot(
            soft[a], stacked(g, a), preferred_element_type=F32
        ).astype(BF16)

    def share_grads(half):
        mine = gv_group.at[half, p]
        for x_ in x_peers:
            send(mine, mine, GV_X + half, device(y, x_, core))
        send(mine, mine, GV_OWN + half, sibling)

    def pass_grads(half):
        wait(gv_group.at[half, 0 : NX - 1], recv_sem.at[GV_X + half])
        for x_ in x_peers:
            theirs = gv_group.at[half, x_ * NC + core]
            send(theirs, theirs, GV_C + half, sibling)

    def turn_tokens(zh):
        wait(tok_group.at[0, 0 : NG // 2], recv_sem.at[TOK + zh])
        lanes = slice((zh % 2) * HD, (zh % 2 + 1) * HD)
        tok_turned[zh] = tok_group[zh // 2, :, :, lanes].reshape(NG * ROWS, HD).T

    for load in loads[:3]:
        load.wait()
    softmax_head(0)
    softmax_head(1)
    share_grads(0)
    softmax_head(2)
    softmax_head(3)
    share_grads(1)
    swap_tokens(1)
    wait(w_far.at[0], recv_sem.at[W_Z])
    for z_lo_ in line_peers:
        send(w_far.at[z_lo], w_far.at[z_lo], W_L, (node_of(y, x, z_lo_, core), z_hi))
    turn_tokens(0)
    pass_grads(0)
    pass_grads(1)
    swap_tokens(2)
    swap_tokens(3)
    for half in range(2):
        wait(gv_group.at[half, 0], recv_sem.at[GV_OWN + half])
        wait(gv_group.at[half, 0 : NX - 1], recv_sem.at[GV_C + half])

    def term_rows(zh):
        for half in range(2):
            term = jnp.dot(
                tok_turned[zh], gv_group[half].reshape(NG * ROWS, KW // 2),
                preferred_element_type=F32,
            )
            term = (term * loss_scale).astype(BF16).reshape(NY, 16, KW // 2)
            part_send[zh, :, :, half * (KW // 2) : (half + 1) * (KW // 2)] = term
        for y_ in y_peers:
            send(part_send.at[zh, y_], part_recv.at[zh, y], PART + zh, device(y_, x, core))
        pltpu.make_async_copy(
            part_send.at[zh, y], part_recv.at[zh, y], recv_sem.at[PART + zh]
        ).start()

    def partial_values(core_):
        total = None
        for pair in range(2):
            left = jnp.concatenate([tok_group[pair, x_ * NC + core_] for x_ in range(NX)], axis=0)
            right = w_cat[2 * pair : 2 * pair + 2].reshape(2 * HD, KW)
            product = jnp.dot(left, right, preferred_element_type=F32)
            total = product if total is None else total + product
        return total.reshape(NX, ROWS, KW)

    gives_own = (lax.rem(y, 2) == z_lo // 2) & (y // 2 == x) & (x * NC + core == y)

    def finish(zh):
        wait(part_recv.at[zh], recv_sem.at[PART + zh])
        part = part_recv[zh, 0].astype(F32)
        for y_ in range(1, NY):
            part = part + part_recv[zh, y_].astype(F32)
        for i in range(4):
            j = zh * 4 + i
            rows = part[4 * i : 4 * i + 4]
            fin_send[j] = jnp.concatenate(
                [rows[:, c * HD : (c + 1) * HD] for c in range(KW // HD)], axis=0
            ).astype(BF16)
            z_lo_, core_ = lax.rem(y, 2) * 2 + i // 2, i % 2
            owner = (node_of(x * NC + core, y // 2, z_lo_, core_), zh)
            own = gives_own & (z_hi == zh) & (z_lo == z_lo_) & (core == core_)

            @pl.when(own)
            def _():
                pltpu.make_async_copy(fin_send.at[j], fin_recv.at[z], recv_sem.at[FIN]).start()

            @pl.when(jnp.logical_not(own))
            def _():
                send(fin_send.at[j], fin_recv.at[z], FIN, owner)

    term_rows(0)
    turn_tokens(1)
    term_rows(1)
    turn_tokens(2)
    term_rows(2)
    finish(0)
    turn_tokens(3)
    term_rows(3)
    wait(w_far.at[0 : NZL - 1], recv_sem.at[W_L])
    loads[3].wait()
    for d, h in enumerate(far_peers):
        w_cat[h] = w_far[:, d].reshape(HD, KW)
    pair_send[...] = partial_values(1 - core).astype(BF16)
    for i, x_ in enumerate(x_peers + [x]):
        send(pair_send.at[x_], pair_recv.at[x_], PAIR + i, sibling)
    val_own[...] = partial_values(core)

    for i, x_ in enumerate(x_peers):
        wait(pair_recv.at[x_], recv_sem.at[PAIR + i])
        val_send[x_] = (val_own[x_] + pair_recv[x_].astype(F32)).astype(BF16)
        for half in range(2):
            lanes = slice(half * (KW // 2), (half + 1) * (KW // 2))
            send(
                val_send.at[x_, :, lanes], val_recv.at[half, x], VAL + half, device(y, x_, core)
            )
    finish(1)
    finish(2)
    finish(3)

    wait(pair_recv.at[x], recv_sem.at[PAIR + NX - 1])
    for half in range(2):
        lanes = slice(half * (KW // 2), (half + 1) * (KW // 2))
        total = val_own[x, :, lanes] + pair_recv[x, :, lanes].astype(F32)
        wait(val_recv.at[half, 0 : NX - 1], recv_sem.at[VAL + half])
        for x_ in x_peers:
            total = total + val_recv[half, x_].astype(F32)
        values = total.astype(BF16)
        for a in (2 * half, 2 * half + 1):
            values_a = values[:, (a % 2) * HD : (a % 2 + 1) * HD]
            grad_scores = []
            for pair in range(GROUP // 2):
                grad_probs = over_columns(values_a, heads(g, a, pair))
                soft_float = soft[a, :, pair * 2 * ROWS : (pair + 1) * 2 * ROWS].astype(F32)
                delta = jnp.sum(soft_float * grad_probs, axis=0, keepdims=True)
                grad_scores.append((soft_float * (grad_probs - delta)).astype(BF16))
            d_keys = jnp.dot(
                jnp.concatenate(grad_scores, axis=1), stacked(q, a), preferred_element_type=F32
            )
            dk_ref[:, a * HD : (a + 1) * HD] = (d_keys * head_scale).astype(BF16)

    wait(fin_recv, recv_sem.at[FIN])
    out = fin_recv[0].astype(F32)
    for z_ in range(1, NZH * NZL):
        out = out + fin_recv[z_].astype(F32)
    for c in range(KW // HD):
        gw_ref[:, c * HD : (c + 1) * HD] = out[4 * c : 4 * c + 4]

    wait(w_far.at[0], send_sem.at[W_Z])
    wait(w_far.at[0 : NZL - 1], send_sem.at[W_L])
    for zh in range(NZH):
        wait(gv_group.at[0, 0:7, :, 0:128], send_sem.at[TOK + zh])
        wait(part_send.at[zh, 0 : NY - 1], send_sem.at[PART + zh])
    for half in range(2):
        wait(gv_group.at[half, 0 : NX - 1], send_sem.at[GV_X + half])
        wait(gv_group.at[half, 0], send_sem.at[GV_OWN + half])
        wait(gv_group.at[half, 0 : NX - 1], send_sem.at[GV_C + half])
        wait(val_recv.at[half, 0 : NX - 1], send_sem.at[VAL + half])
    for i in range(NX):
        wait(pair_send.at[0], send_sem.at[PAIR + i])
    wait(fin_send.at[0:15], send_sem.at[FIN])

    @pl.when(jnp.logical_not(gives_own))
    def _():
        wait(fin_send.at[0], send_sem.at[FIN])


def shards(tokens, queries, keys, grad_attended, w_value):
    total_tokens = lax.axis_size("node") * lax.axis_size("local") * tokens.shape[0]
    loss_scale = float(total_tokens) ** -0.5

    def body(*refs):
        kernel(*refs, loss_scale=loss_scale)

    return pl.pallas_call(
        body,
        out_shape=(
            pltpu.VMEM((ROWS, KW), BF16),
            pltpu.VMEM((4, KW), F32),
        ),
        in_specs=[pl.BlockSpec(memory_space=pl.ANY)] * 5,
        out_specs=(pl.BlockSpec(memory_space=pltpu.VMEM),) * 2,
        scratch_shapes=[
            pltpu.VMEM((ROWS, 4096), BF16),
            pltpu.VMEM((ROWS, KW), BF16),
            pltpu.VMEM((ROWS, 4096), BF16),
            pltpu.VMEM((NZL, NZH - 1, 32, KW), BF16),
            pltpu.VMEM((NZH, HD, KW), BF16),
            pltpu.VMEM((KVH, ROWS, GROUP * ROWS), BF16),
            pltpu.VMEM((2, NG, ROWS, 2 * HD), BF16),
            pltpu.VMEM((NZH, HD, NG * ROWS), BF16),
            pltpu.VMEM((2, NG, ROWS, KW // 2), BF16),
            pltpu.VMEM((NZH, NY, 16, KW), BF16),
            pltpu.VMEM((NZH, NY, 16, KW), BF16),
            pltpu.VMEM((16, 16, HD), BF16),
            pltpu.VMEM((16, 16, HD), BF16),
            pltpu.VMEM((NX, ROWS, KW), BF16),
            pltpu.VMEM((NX, ROWS, KW), BF16),
            pltpu.VMEM((NX, ROWS, KW), F32),
            pltpu.VMEM((NX, ROWS, KW), BF16),
            pltpu.VMEM((2, NX, ROWS, KW // 2), BF16),
            pltpu.SemaphoreType.DMA((4,)),
            pltpu.SemaphoreType.DMA((23,)),
            pltpu.SemaphoreType.DMA((23,)),
        ],
        compiler_params=pltpu.CompilerParams(
            collective_id=0, has_side_effects=True, vmem_limit_bytes=60 * 1024 * 1024
        ),
        cost_estimate=pl.CostEstimate(
            flops=1_700_000_000, bytes_accessed=5_000_000, transcendentals=524_288
        ),
    )(tokens, queries, keys, grad_attended, w_value)


def solution(mesh):
    in_specs = (
        P(("node", "local"), None),
        P(("node", "local"), None),
        P(("node", "local"), None),
        P(("node", "local"), None),
        P("local", None),
    )
    out_specs = (P(("node", "local"), None), P(("local", "node"), None))
    return jax.shard_map(shards, mesh=mesh, in_specs=in_specs, out_specs=out_specs, check_vma=False)
```

```python
import jax
import jax.numpy as jnp
from jax import lax
from jax.experimental import pallas as pl
from jax.experimental.pallas import tpu as pltpu
from jax.sharding import PartitionSpec as P

HD = 128
KVH = 4
GROUP = 8
ROWS = 128
KW = 512
NX, NY, NZL, NZH, NC = 4, 8, 4, 4, 2
NG = NX * NC
W_Z, W_L, FIN, GV_X, GV_OWN, GV_C, VAL, TOK, PART, PAIR = 0, 1, 2, 3, 5, 7, 9, 11, 15, 19
LOG2_E = 1.4426950408889634
MESH = pl.DeviceIdType.MESH
F32 = jnp.float32
BF16 = jnp.bfloat16


def node_of(y, x, z_lo, core):
    return ((y * NX + x) * NZL + z_lo) * NC + core


def over_columns(left, right):
    return lax.dot_general(left, right, (((1,), (1,)), ((), ())), preferred_element_type=F32)


def stacked(ref, a):
    return jnp.concatenate(
        [ref[:, (a * GROUP + g) * HD : (a * GROUP + g + 1) * HD] for g in range(GROUP)], axis=0
    )


def kernel(
    tok_hbm, q_hbm, k_hbm, g_hbm, w_hbm, dk_ref, gw_ref,
    q, k, g, w_far, w_cat, soft, tok_group, tok_turned, gv_group, part_send, part_recv,
    fin_send, fin_recv, pair_send, pair_recv, val_own, val_send, val_recv,
    load_sem, send_sem, recv_sem, *, loss_scale,
):
    node, z_hi = lax.axis_index("node"), lax.axis_index("local")
    core = lax.rem(node, NC)
    z_lo = lax.rem(node // NC, NZL)
    x = lax.rem(node // (NC * NZL), NX)
    y = node // (NC * NZL * NX)
    z = z_hi * NZL + z_lo
    p = x * NC + core
    head_scale = float(HD) ** -0.5

    def device(y_, x_, core_):
        return (node_of(y_, x_, z_lo, core_), z_hi)

    sibling = device(y, x, 1 - core)
    x_peers = [lax.rem(x + d, NX) for d in (2, 1, 3)]
    y_peers = [lax.rem(y + d, NY) for d in range(1, NY)]
    line_peers = [lax.rem(z_lo + d, NZL) for d in range(1, NZL)]
    far_peers = [lax.rem(z_hi + d, NZH) for d in range(1, NZH)]

    own_rows = w_hbm.at[pl.ds(pl.multiple_of(p * HD, HD), HD)]
    loads = [
        pltpu.make_async_copy(src, dst, load_sem.at[i])
        for i, (src, dst) in enumerate(
            [(q_hbm, q), (k_hbm, k), (g_hbm, g), (own_rows, w_cat.at[z_hi])]
        )
    ]
    for load in loads:
        load.start()

    barrier = pltpu.get_barrier_semaphore()

    def greet(device_id):
        pl.semaphore_signal(barrier, inc=1, device_id=device_id, device_id_type=MESH)

    giver_y, giver_x, giver_core = x * 2 + z_lo // 2, y // 2, lax.rem(y, 2)
    takes_own = (giver_y == y) & (giver_x == x) & (giver_core == core)
    for z_ in range(NZH * NZL):
        giver = (node_of(giver_y, giver_x, z_ % NZL, giver_core), z_ // NZL)

        @pl.when(jnp.logical_not(takes_own & (z == z_)))
        def _():
            greet(giver)

    for h in far_peers:
        greet((node, h))
    for z_lo_ in line_peers:
        greet((node_of(y, x, z_lo_, core), z_hi))
    for y_ in y_peers:
        greet(device(y_, x, core))
    for x_ in x_peers:
        for core_ in (core, 1 - core):
            greet(device(y, x_, core_))
    greet(sibling)
    near = 1 + 2 * (NX - 1) + (NY - 1) + (NZH - 1) + (NZL - 1)
    pl.semaphore_wait(barrier, near + NZH * NZL - jnp.where(takes_own, 1, 0))

    def send(src, dst, phase, device_id):
        pltpu.make_async_remote_copy(
            src_ref=src, dst_ref=dst, send_sem=send_sem.at[phase], recv_sem=recv_sem.at[phase],
            device_id=device_id, device_id_type=MESH,
        ).start()

    def wait(ref, sem):
        pltpu.make_async_copy(ref, ref, sem).wait()

    piece = w_hbm.at[pl.ds(pl.multiple_of(p * HD + z_lo * 32, 32), 32)]
    for d, h in enumerate(far_peers):
        send(piece, w_far.at[z_lo, NZH - 2 - d], W_Z, (node, h))

    def columns(zh, p_):
        return tok_hbm.at[:, pl.ds(pl.multiple_of(zh * (NG * HD) + p_ * HD, HD), HD)]

    def place(zh):
        return tok_group.at[zh // 2, p, :, (zh % 2) * HD : (zh % 2 + 1) * HD]

    def swap_tokens(zh):
        for x_ in x_peers:
            for core_ in (core, 1 - core):
                send(columns(zh, x_ * NC + core_), place(zh), TOK + zh, device(y, x_, core_))
        send(columns(zh, x * NC + 1 - core), place(zh), TOK + zh, sibling)
        pltpu.make_async_copy(columns(zh, p), place(zh), recv_sem.at[TOK + zh]).start()

    swap_tokens(0)

    key_ids = lax.broadcasted_iota(jnp.int32, (ROWS, 2 * ROWS), 0)
    lane_ids = lax.broadcasted_iota(jnp.int32, (ROWS, 2 * ROWS), 1)
    allowed = key_ids <= lax.rem(lane_ids, ROWS)
    exponent_scale = head_scale * LOG2_E

    def heads(ref, a, pair):
        first = a * GROUP + 2 * pair
        return jnp.concatenate(
            [ref[:, h * HD : (h + 1) * HD] for h in (first, first + 1)], axis=0
        )

    def softmax_head(a):
        cols = slice(a * HD, (a + 1) * HD)
        keys_a = k[:, cols]
        for pair in range(GROUP // 2):
            scores = over_columns(keys_a, heads(q, a, pair))
            scores = jnp.where(allowed, scores, F32(-1e30))
            peak = jnp.max(scores, axis=0, keepdims=True)
            raised = jnp.exp2((scores - peak) * exponent_scale)
            inverse = 1.0 / jnp.sum(raised, axis=0, keepdims=True)
            soft[a, :, pair * 2 * ROWS : (pair + 1) * 2 * ROWS] = (raised * inverse).astype(BF16)
        gv_group[a // 2, p, :, (a % 2) * HD : (a % 2 + 1) * HD] = jnp.dot(
            soft[a], stacked(g, a), preferred_element_type=F32
        ).astype(BF16)

    def share_grads(half):
        mine = gv_group.at[half, p]
        for x_ in x_peers:
            send(mine, mine, GV_X + half, device(y, x_, core))
        send(mine, mine, GV_OWN + half, sibling)

    def pass_grads(half):
        wait(gv_group.at[half, 0 : NX - 1], recv_sem.at[GV_X + half])
        for x_ in x_peers:
            theirs = gv_group.at[half, x_ * NC + core]
            send(theirs, theirs, GV_C + half, sibling)

    def turn_tokens(zh):
        wait(tok_group.at[0, 0 : NG // 2], recv_sem.at[TOK + zh])
        lanes = slice((zh % 2) * HD, (zh % 2 + 1) * HD)
        tok_turned[zh] = tok_group[zh // 2, :, :, lanes].reshape(NG * ROWS, HD).T

    for load in loads[:3]:
        load.wait()
    softmax_head(0)
    softmax_head(1)
    share_grads(0)
    softmax_head(2)
    softmax_head(3)
    share_grads(1)
    swap_tokens(1)
    wait(w_far.at[0], recv_sem.at[W_Z])
    for z_lo_ in line_peers:
        send(w_far.at[z_lo], w_far.at[z_lo], W_L, (node_of(y, x, z_lo_, core), z_hi))
    turn_tokens(0)
    pass_grads(0)
    pass_grads(1)
    swap_tokens(2)
    swap_tokens(3)
    for half in range(2):
        wait(gv_group.at[half, 0], recv_sem.at[GV_OWN + half])
        wait(gv_group.at[half, 0 : NX - 1], recv_sem.at[GV_C + half])

    def term_rows(zh):
        for half in range(2):
            term = jnp.dot(
                tok_turned[zh], gv_group[half].reshape(NG * ROWS, KW // 2),
                preferred_element_type=F32,
            )
            term = (term * loss_scale).astype(BF16).reshape(NY, 16, KW // 2)
            part_send[zh, :, :, half * (KW // 2) : (half + 1) * (KW // 2)] = term
        for y_ in y_peers:
            send(part_send.at[zh, y_], part_recv.at[zh, y], PART + zh, device(y_, x, core))
        pltpu.make_async_copy(
            part_send.at[zh, y], part_recv.at[zh, y], recv_sem.at[PART + zh]
        ).start()

    def partial_values(core_):
        total = None
        for pair in range(2):
            left = jnp.concatenate([tok_group[pair, x_ * NC + core_] for x_ in range(NX)], axis=0)
            right = w_cat[2 * pair : 2 * pair + 2].reshape(2 * HD, KW)
            product = jnp.dot(left, right, preferred_element_type=F32)
            total = product if total is None else total + product
        return total.reshape(NX, ROWS, KW)

    gives_own = (lax.rem(y, 2) == z_lo // 2) & (y // 2 == x) & (x * NC + core == y)

    def finish(zh):
        wait(part_recv.at[zh], recv_sem.at[PART + zh])
        part = part_recv[zh, 0].astype(F32)
        for y_ in range(1, NY):
            part = part + part_recv[zh, y_].astype(F32)
        for i in range(4):
            j = zh * 4 + i
            rows = part[4 * i : 4 * i + 4]
            fin_send[j] = jnp.concatenate(
                [rows[:, c * HD : (c + 1) * HD] for c in range(KW // HD)], axis=0
            ).astype(BF16)
            z_lo_, core_ = lax.rem(y, 2) * 2 + i // 2, i % 2
            owner = (node_of(x * NC + core, y // 2, z_lo_, core_), zh)
            own = gives_own & (z_hi == zh) & (z_lo == z_lo_) & (core == core_)

            @pl.when(own)
            def _():
                pltpu.make_async_copy(fin_send.at[j], fin_recv.at[z], recv_sem.at[FIN]).start()

            @pl.when(jnp.logical_not(own))
            def _():
                send(fin_send.at[j], fin_recv.at[z], FIN, owner)

    term_rows(0)
    turn_tokens(1)
    term_rows(1)
    turn_tokens(2)
    term_rows(2)
    finish(0)
    turn_tokens(3)
    term_rows(3)
    wait(w_far.at[0 : NZL - 1], recv_sem.at[W_L])
    loads[3].wait()
    for d, h in enumerate(far_peers):
        w_cat[h] = w_far[:, d].reshape(HD, KW)
    pair_send[...] = partial_values(1 - core).astype(BF16)
    for i, x_ in enumerate(x_peers + [x]):
        send(pair_send.at[x_], pair_recv.at[x_], PAIR + i, sibling)
    val_own[...] = partial_values(core)

    for i, x_ in enumerate(x_peers):
        wait(pair_recv.at[x_], recv_sem.at[PAIR + i])
        val_send[x_] = (val_own[x_] + pair_recv[x_].astype(F32)).astype(BF16)
        for half in range(2):
            lanes = slice(half * (KW // 2), (half + 1) * (KW // 2))
            send(
                val_send.at[x_, :, lanes], val_recv.at[half, x], VAL + half, device(y, x_, core)
            )
    finish(1)
    finish(2)
    finish(3)

    wait(pair_recv.at[x], recv_sem.at[PAIR + NX - 1])
    for half in range(2):
        lanes = slice(half * (KW // 2), (half + 1) * (KW // 2))
        total = val_own[x, :, lanes] + pair_recv[x, :, lanes].astype(F32)
        wait(val_recv.at[half, 0 : NX - 1], recv_sem.at[VAL + half])
        for x_ in x_peers:
            total = total + val_recv[half, x_].astype(F32)
        values = total.astype(BF16)
        for a in (2 * half, 2 * half + 1):
            values_a = values[:, (a % 2) * HD : (a % 2 + 1) * HD]
            grad_scores = []
            for pair in range(GROUP // 2):
                grad_probs = over_columns(values_a, heads(g, a, pair))
                soft_float = soft[a, :, pair * 2 * ROWS : (pair + 1) * 2 * ROWS].astype(F32)
                delta = jnp.sum(soft_float * grad_probs, axis=0, keepdims=True)
                grad_scores.append((soft_float * (grad_probs - delta)).astype(BF16))
            d_keys = jnp.dot(
                jnp.concatenate(grad_scores, axis=1), stacked(q, a), preferred_element_type=F32
            )
            dk_ref[:, a * HD : (a + 1) * HD] = (d_keys * head_scale).astype(BF16)

    wait(fin_recv, recv_sem.at[FIN])
    out = fin_recv[0].astype(F32)
    for z_ in range(1, NZH * NZL):
        out = out + fin_recv[z_].astype(F32)
    for c in range(KW // HD):
        gw_ref[:, c * HD : (c + 1) * HD] = out[4 * c : 4 * c + 4]

    wait(w_far.at[0], send_sem.at[W_Z])
    wait(w_far.at[0 : NZL - 1], send_sem.at[W_L])
    for zh in range(NZH):
        wait(gv_group.at[0, 0:7, :, 0:128], send_sem.at[TOK + zh])
        wait(part_send.at[zh, 0 : NY - 1], send_sem.at[PART + zh])
    for half in range(2):
        wait(gv_group.at[half, 0 : NX - 1], send_sem.at[GV_X + half])
        wait(gv_group.at[half, 0], send_sem.at[GV_OWN + half])
        wait(gv_group.at[half, 0 : NX - 1], send_sem.at[GV_C + half])
        wait(val_recv.at[half, 0 : NX - 1], send_sem.at[VAL + half])
    for i in range(NX):
        wait(pair_send.at[0], send_sem.at[PAIR + i])
    wait(fin_send.at[0:15], send_sem.at[FIN])

    @pl.when(jnp.logical_not(gives_own))
    def _():
        wait(fin_send.at[0], send_sem.at[FIN])


def shards(tokens, queries, keys, grad_attended, w_value):
    total_tokens = lax.axis_size("node") * lax.axis_size("local") * tokens.shape[0]
    loss_scale = float(total_tokens) ** -0.5

    def body(*refs):
        kernel(*refs, loss_scale=loss_scale)

    return pl.pallas_call(
        body,
        out_shape=(
            pltpu.VMEM((ROWS, KW), BF16),
            pltpu.VMEM((4, KW), F32),
        ),
        in_specs=[pl.BlockSpec(memory_space=pl.ANY)] * 5,
        out_specs=(pl.BlockSpec(memory_space=pltpu.VMEM),) * 2,
        scratch_shapes=[
            pltpu.VMEM((ROWS, 4096), BF16),
            pltpu.VMEM((ROWS, KW), BF16),
            pltpu.VMEM((ROWS, 4096), BF16),
            pltpu.VMEM((NZL, NZH - 1, 32, KW), BF16),
            pltpu.VMEM((NZH, HD, KW), BF16),
            pltpu.VMEM((KVH, ROWS, GROUP * ROWS), BF16),
            pltpu.VMEM((2, NG, ROWS, 2 * HD), BF16),
            pltpu.VMEM((NZH, HD, NG * ROWS), BF16),
            pltpu.VMEM((2, NG, ROWS, KW // 2), BF16),
            pltpu.VMEM((NZH, NY, 16, KW), BF16),
            pltpu.VMEM((NZH, NY, 16, KW), BF16),
            pltpu.VMEM((16, 16, HD), BF16),
            pltpu.VMEM((16, 16, HD), BF16),
            pltpu.VMEM((NX, ROWS, KW), BF16),
            pltpu.VMEM((NX, ROWS, KW), BF16),
            pltpu.VMEM((NX, ROWS, KW), F32),
            pltpu.VMEM((NX, ROWS, KW), BF16),
            pltpu.VMEM((2, NX, ROWS, KW // 2), BF16),
            pltpu.SemaphoreType.DMA((4,)),
            pltpu.SemaphoreType.DMA((23,)),
            pltpu.SemaphoreType.DMA((23,)),
        ],
        compiler_params=pltpu.CompilerParams(
            collective_id=0, has_side_effects=True, vmem_limit_bytes=60 * 1024 * 1024
        ),
        cost_estimate=pl.CostEstimate(
            flops=1_700_000_000, bytes_accessed=5_000_000, transcendentals=524_288
        ),
    )(tokens, queries, keys, grad_attended, w_value)


def solution(mesh):
    in_specs = (
        P(("node", "local"), None),
        P(("node", "local"), None),
        P(("node", "local"), None),
        P(("node", "local"), None),
        P("local", None),
    )
    out_specs = (P(("node", "local"), None), P(("local", "node"), None))
    return jax.shard_map(shards, mesh=mesh, in_specs=in_specs, out_specs=out_specs, check_vma=False)
```
